32 devices in a mesh: groups: 2 (over y), owners: 4 (over z), section: 2 (over x), rep: 2 (over core).
Axes of the slice: x: 2, y: 2, z: 4, core: 2. Of those that a mesh axis runs over, the one named last changes fastest.
Arguments:
- inputs: bfloat16 [2, 4096, 512], P('section', 'owners', ('groups', 'rep')), parts along dimension 2, may hold values from -6 to 6
- weight_first: bfloat16 [2, 32, 2048, 128], P('section', ('owners', 'rep')), may hold values from -0.1875 to 0.1875
- weight_second: bfloat16 [2, 32, 1024, 128], P('section', ('owners', 'rep')), may hold values from -0.25 to 0.25
- bias_first: float32 [2, 4096], P('section', 'owners'), may hold values from -1.5 to 1.5
- bias_second: float32 [2, 4096], P('section', 'owners'), may hold values from -1.5 to 1.5
- links_first: int32 [2, 32, 16], P('section', 'owners'), may hold values from 0 to 15, as said below
- links_second: int32 [2, 32, 8], P('section', 'owners'), may hold values from 0 to 7, as said below
Outputs:
- final_activity: bfloat16 [2, 4096, 512], P('section', 'owners', ('groups', 'rep')), parts along dimension 2
The draws below stay inside these ranges and needn't reach their ends.
There are 2 independent parts, one for each index of `groups`. The reference program is written for one: setup_inputs(seed, part) draws one part's arguments, and reference() takes and returns one part's arrays. A program takes and returns all parts, laid end to end along the dimension named above; an argument that names none is the same for every part. Nothing has to cross between parts.
Inputs may be any that keep to these rules, and one draw needn't show every extreme that they name: `links_first`: in every row of every section the 16 entries are distinct. `links_second`: in every row of every section the 8 entries are distinct.
All inputs are finite; a program needn't handle non-finite values.
Results may differ from the reference program's by a relative error of at most 0.014.
Values may be sent and summed in bfloat16 or wider, within the bound.
No kernel may reach another device: no remote copies, remote signals or barrier semaphores. Data moves between devices by JAX's collectives and lax.ppermute only.
A program may use at most 64 MiB of HBM per device.

```python
import jax
import jax.numpy as jnp
from jax import lax

BLOCK = 128
RADIX_A = 16
RADIX_B = 8
NN = 4096
NB = 32
BATCH = 256
MICRO = 2
N_OWNERS = 4
N_SECTION = 2


def draw_links_first(key, part):
    key_list = jax.random.split(jax.random.fold_in(key, 11), N_SECTION * NB)
    shuffled = jax.vmap(lambda subkey: jax.random.permutation(subkey, RADIX_A))(key_list)
    return shuffled.reshape(N_SECTION, NB, RADIX_A).astype(jnp.int32)


def draw_links_second(key, part):
    key_list = jax.random.split(jax.random.fold_in(key, 23), N_SECTION * NB)
    shuffled = jax.vmap(lambda subkey: jax.random.permutation(subkey, RADIX_B))(key_list)
    return shuffled.reshape(N_SECTION, NB, RADIX_B).astype(jnp.int32)


def level_of(own_key, dims, cuts, smallest, high):
    loudness = 1.0
    for dim, parts in cuts:
        draws = jax.random.uniform(jax.random.fold_in(jax.random.fold_in(own_key, 6), dim), (parts,), jnp.float32, smallest / len(cuts), high / len(cuts))
        loudness = loudness * jnp.repeat(jnp.exp(draws), dims[dim] // parts).reshape((-1,) + (1,) * (len(dims) - 1 - dim))
    return loudness


def scatter_about(stream_key, extent, width, limit, cuts=(), kind=jnp.bfloat16):
    array = width * jax.random.normal(stream_key, extent, jnp.float32)
    if cuts:
        array = array * level_of(stream_key, extent, cuts, -0.22, 0.18)
    return jnp.clip(array, -limit, limit).astype(kind)


def setup_inputs(seed: int = 0, part: int = 0) -> dict:
    key_of = jax.random.split(jax.random.key(seed), 8)
    part_splits = jax.random.split(jax.random.fold_in(key_of[7], part), 8)
    inputs = scatter_about(part_splits[0], (MICRO, NN, BATCH), 1.0, 6.0, ((0, 2), (1, 4), (2, 2)))
    weight_first = scatter_about(key_of[1], (N_SECTION, NB, RADIX_A * BLOCK, BLOCK), (RADIX_A * BLOCK // 2) ** -0.5, 0.1875, ((0, 2), (1, 8)))
    weight_second = scatter_about(key_of[2], (N_SECTION, NB, RADIX_B * BLOCK, BLOCK), (RADIX_B * BLOCK // 2) ** -0.5, 0.25, ((0, 2), (1, 8)))
    bias_first = scatter_about(key_of[3], (N_SECTION, NN), 0.3, 1.5, ((0, 2), (1, 4)), jnp.float32)
    bias_second = scatter_about(key_of[4], (N_SECTION, NN), 0.3, 1.5, ((0, 2), (1, 4)), jnp.float32)
    links_first = draw_links_first(jax.random.fold_in(key_of[7], 71), part)
    links_second = draw_links_second(jax.random.fold_in(key_of[7], 71), part)
    return {"inputs": inputs, "weight_first": weight_first, "weight_second": weight_second, "bias_first": bias_first, "bias_second": bias_second, "links_first": links_first, "links_second": links_second}


CEILING = 4.0


def regroup(activity):
    owner_width = activity.shape[0] // N_OWNERS
    piece_len = owner_width // N_OWNERS
    batch_len = activity.shape[1]
    shaped = activity.reshape(N_OWNERS, N_OWNERS, piece_len, batch_len)
    return jnp.transpose(shaped, (1, 0, 2, 3)).reshape(activity.shape)


def radix_layer(activity, tiles, link_table, bias_row):
    radix_len = link_table.shape[1]
    groups_total = link_table.shape[0] // radix_len
    tile_size = tiles.shape[2]
    batch_len = activity.shape[1]
    grouped_act = activity.reshape(groups_total, radix_len, tile_size, batch_len)
    grouped_tiles = tiles.reshape(groups_total, radix_len, radix_len * tile_size, tile_size)
    grouped_links = link_table.reshape(groups_total, radix_len, radix_len)
    grouped_bias = bias_row.reshape(groups_total, radix_len, tile_size)

    def one_group(packed):
        blocks, tile_group, link_group, bias_group = packed
        picked = jnp.take(blocks, link_group, axis=0)
        picked = picked.reshape(radix_len, radix_len * tile_size, batch_len).astype(jnp.float32)
        summed = jnp.einsum("bkc,bkr->bcr", tile_group.astype(jnp.float32), picked,
                            precision=lax.Precision.HIGHEST)
        summed = summed + bias_group[:, :, None]
        return jnp.clip(summed, 0.0, CEILING).astype(jnp.bfloat16)

    mapped = lax.map(one_group, (grouped_act, grouped_tiles, grouped_links, grouped_bias))
    return mapped.reshape(link_table.shape[0] * tile_size, batch_len)


def reference(inputs, weight_first, weight_second, bias_first, bias_second, links_first, links_second):
    results = []
    for micro_idx in range(MICRO):
        activity = inputs[micro_idx]
        for section_pos in range(N_SECTION):
            activity = radix_layer(regroup(activity), weight_first[section_pos], links_first[section_pos], bias_first[section_pos])
            activity = radix_layer(regroup(activity), weight_second[section_pos], links_second[section_pos], bias_second[section_pos])
        results.append(activity)
    return jnp.stack(results)
```

```python
import functools

import jax
import jax.numpy as jnp
from jax import lax
from jax.experimental import pallas as pl
from jax.experimental.pallas import tpu as pltpu
from jax.sharding import PartitionSpec as P

CEILING = 4.0


def layer_kernel(
    tile_list, out_groups, neuron_major, final, active_section, *refs
):
    meta, table, own_tiles, other_tiles, bias = refs[:5]
    buffer_count = 1 + max(buffer for buffer, _ in tile_list)
    buffers = refs[5 : 5 + buffer_count]
    rest = list(refs[5 + buffer_count :])
    settled = rest.pop(0) if final == "merge" else None
    out_count = 1 if final else len(out_groups)
    outs = rest[:out_count]
    tiles, turned, arrivals = rest[out_count:]
    me, rep, section = meta[0], meta[1], meta[2]
    half = own_tiles.shape[0]
    size = tiles.shape[2]
    width = 2 * size

    def run():
        for base, source in ((rep * half, own_tiles), ((1 - rep) * half, other_tiles)):
            for low in range(0, half, 2):
                pltpu.make_async_copy(
                    source.at[pl.ds(low, 2)],
                    tiles.at[pl.ds(base + low, 2)],
                    arrivals.at[(base + low) // 2],
                ).start()
        if neuron_major:
            for place, (buffer, column) in enumerate(tile_list):
                turned[place] = buffers[buffer][pl.ds(column, width), :].T
        for distance in range(2 * half // 2):
            owner = me ^ distance
            pltpu.make_async_copy(
                own_tiles.at[pl.ds(0, 2)], tiles.at[pl.ds(2 * owner, 2)], arrivals.at[owner]
            ).wait()
            rows = turned.shape[1]
            total = jnp.zeros((rows, width), jnp.float32)
            for place, (buffer, column) in enumerate(tile_list):
                if neuron_major:
                    left = turned[place]
                else:
                    left = buffers[buffer][:, pl.ds(column, width)]
                right = jnp.concatenate(
                    [
                        jnp.concatenate(
                            [
                                tiles[
                                    2 * owner + j,
                                    pl.ds(
                                        pl.multiple_of(table[2 * distance + j, 2 * place + i] * size, size),
                                        size,
                                    ),
                                    :,
                                ]
                                for j in range(2)
                            ],
                            axis=1,
                        )
                        for i in range(2)
                    ],
                    axis=0,
                )
                total = total + jnp.dot(left, right, preferred_element_type=jnp.float32)
            shift = jnp.concatenate([bias[pl.ds(2 * owner + j, 1), :] for j in range(2)], axis=1)
            value = jnp.clip(total + shift, 0.0, CEILING)
            if final:
                outs[0][pl.ds(pl.multiple_of(owner * width, width), width), :] = value.T.astype(jnp.bfloat16)
            else:
                for out, group in zip(outs, out_groups, strict=True):
                    if distance in group:
                        out[:, pl.ds(group.index(distance) * width, width)] = value.astype(jnp.bfloat16)

    pl.when(section == active_section)(run)
    if final == "merge":

        @pl.when(section != active_section)
        def _():
            outs[0][...] = settled[...]


def layer(
    meta, table, own_tiles, other_tiles, bias, buffers, tile_list, out_groups, active_section,
    neuron_major=False, final=None, settled=None,
):
    half, depth, size = own_tiles.shape
    rows = buffers[0].shape[1] if neuron_major else buffers[0].shape[0]
    if final:
        shapes = [jax.ShapeDtypeStruct((2 * half * size, rows), jnp.bfloat16)]
    else:
        shapes = [jax.ShapeDtypeStruct((rows, len(group) * 2 * size), jnp.bfloat16) for group in out_groups]
    smem = pl.BlockSpec(memory_space=pltpu.SMEM)
    hbm = pl.BlockSpec(memory_space=pl.ANY)
    vmem = pl.BlockSpec(memory_space=pltpu.VMEM)
    operands = [meta, table, own_tiles, other_tiles, bias, *buffers] + ([settled] if final == "merge" else [])
    turned = (len(tile_list), rows, 2 * size) if neuron_major else (1, rows, 2 * size)
    return pl.pallas_call(
        functools.partial(layer_kernel, tile_list, out_groups, neuron_major, final, active_section),
        out_shape=shapes,
        in_specs=[smem, smem, hbm, hbm] + [vmem] * (len(operands) - 4),
        out_specs=[vmem] * len(shapes),
        scratch_shapes=[
            pltpu.VMEM((2 * half, depth, size), jnp.bfloat16),
            pltpu.VMEM(turned, jnp.bfloat16),
            pltpu.SemaphoreType.DMA((half,)),
        ],
        compiler_params=pltpu.CompilerParams(vmem_limit_bytes=24 * 2**20),
        cost_estimate=pl.CostEstimate(
            flops=4 * half * depth * size * rows, bytes_accessed=4 * half * depth * size, transcendentals=0
        ),
    )(*operands)


def fast_body(inputs, weight_first, weight_second, bias_first, bias_second, links_first, links_second):
    owner_count = lax.axis_size("owners")
    section = lax.axis_index("section")
    me = lax.axis_index("owners")
    rep = lax.axis_index("rep")
    size = weight_first.shape[3]
    features = inputs[0]
    piece = features.shape[0] // owner_count
    meta = jnp.stack([me, rep, section]).astype(jnp.int32)

    def moved(value, distance, cross):
        pairs = []
        for owner in range(owner_count):
            for place in range(2):
                target = (owner ^ distance) * 2 + (1 - place if cross else place)
                pairs.append((owner * 2 + place, target))
        return lax.ppermute(value, ("owners", "section"), pairs)

    def other_core(value):
        return lax.ppermute(value, "rep", [(0, 1), (1, 0)])

    def table_of(links, places):
        count = links.shape[0]
        order = jnp.arange(count)
        wanted = 2 * (me ^ (order // 2)) + order % 2
        slots = jnp.arange(links.shape[1])
        row = wanted[:, None, None, None] == jnp.arange(count)[None, None, :, None]
        hit = links[None, None, :, :] == places[None, :, None, None]
        return jnp.sum(jnp.where(row & hit, slots[None, None, None, :], 0), axis=(2, 3)).astype(jnp.int32)

    def first_places(sources):
        found = []
        for source, target in sources:
            low = ((me ^ target) % 2) * (owner_count * 2) + (me ^ source) * 2
            found += [low, low + 1]
        return jnp.stack(found)

    features = features.reshape(owner_count, piece, features.shape[1])
    cut = [lax.dynamic_index_in_dim(features, me ^ distance, 0, keepdims=False) for distance in range(owner_count)]
    near = jnp.concatenate(cut[:2], axis=0)
    far = jnp.concatenate(cut[2:], axis=0)
    start = [near, moved(near, 1, False), moved(far, 2, False), moved(far, 3, False)]
    first_own, second_own = weight_first[0], weight_second[0]
    first_other = other_core(first_own)
    second_other = other_core(second_own)
    later = [moved(value, 0, True) for value in start]

    direct = [(0, 0), (0, 1), (1, 1), (1, 0), (2, 0), (2, 1), (3, 1), (3, 0)]
    direct_tiles = [(buffer, column * piece) for buffer in range(4) for column in range(2)]
    relayed = [(0, 0), (0, 1), (1, 1), (1, 0), (2, 0), (3, 0), (3, 1), (2, 1)]
    relayed_tiles = [(0, 0), (0, piece), (1, 0), (1, piece), (2, 0), (3, 0), (4, 0), (5, 0)]
    second_tiles = [(buffer, 0) for buffer in range(4)]

    direct_table = table_of(links_first[0], first_places(direct))
    relayed_table = table_of(links_first[0], first_places(relayed))
    second_places = jnp.stack([2 * (me ^ (place // 2)) + place % 2 for place in range(2 * owner_count)])
    second_table = table_of(links_second[0], second_places)
    first_bias = bias_first[0].reshape(-1, size)
    second_bias = bias_second[0].reshape(-1, size)

    apart = [[0], [1], [2], [3]]
    joined = [[0, 1], [2], [3]]

    def first_layer(buffers, active, raw):
        return layer(
            meta, direct_table if raw else relayed_table, first_own, first_other, first_bias, buffers,
            direct_tiles if raw else relayed_tiles, apart, active, neuron_major=raw,
        )

    def second_layer(parts, active, **more):
        buffers = [parts[0]] + [moved(parts[distance], distance, False) for distance in range(1, owner_count)]
        return layer(
            meta, second_table, second_own, second_other, second_bias, buffers, second_tiles, joined, active, **more
        )

    def hand_over(result):
        close, far_two, far_three = result
        two, three = moved(far_two, 2, True), moved(far_three, 3, True)
        close = moved(close, 0, True)
        return [close, moved(close, 1, False), two, three, moved(two, 1, False), moved(three, 1, False)]

    zero = second_layer(first_layer(start, 0, True), 0)
    one = second_layer(first_layer(later, 0, True), 0)
    settled = second_layer(first_layer(hand_over(zero), 1, False), 1, final="plain")[0]
    settled = moved(settled, 0, True)
    return second_layer(first_layer(hand_over(one), 1, False), 1, final="merge", settled=settled)[0][None]


def from_behind(value, axis, steps):
    count = lax.axis_size(axis)
    pairs = [(source, (source + steps) % count) for source in range(count)]
    return lax.ppermute(value, axis, pairs)


def swapped(block, axis, distance):
    count = lax.axis_size(axis)
    route = []
    for low in range(count):
        high = low | 1 << distance
        if high != low and high < count:
            route += [(low, high), (high, low)]
    return lax.ppermute(block, axis, route)


def passed_along(array, axis, by):
    size = lax.axis_size(axis)
    pairs = [(i, i + by) for i in range(size) if 0 <= i + by < size]
    return lax.ppermute(array, axis, pairs)


def order_tiles(tiles, link_table):
    block_count = tiles.shape[0]
    radix_len = link_table.shape[1]
    tile_size = tiles.shape[2]
    inverse = jnp.argsort(link_table, axis=1)
    shaped = tiles.reshape(block_count, radix_len, tile_size, tile_size)
    ordered = jnp.take_along_axis(shaped, inverse[:, :, None, None], axis=1)
    return ordered.reshape(block_count, radix_len * tile_size, tile_size)


def mixed_layer(group_rows, ordered, bias_row):
    block_count = ordered.shape[0]
    tile_size = ordered.shape[2]
    row_count = group_rows.shape[1]
    summed = jnp.einsum("bkc,kr->bcr", ordered, group_rows, preferred_element_type=jnp.float32)
    summed = summed.reshape(block_count * tile_size, row_count) + bias_row[:, None]
    return jnp.clip(summed, 0.0, CEILING).astype(jnp.bfloat16)


def rotate_slots(slot_store):
    return from_behind(slot_store, "section", 1)


def general_body(inputs, weight_first, weight_second, bias_first, bias_second, links_first, links_second):
    section_count = lax.axis_size("section")
    section_here = lax.axis_index("section")
    owner_parity = lax.axis_index("owners") % 2
    slot_store = inputs[0]
    row_count = slot_store.shape[1]
    owner_width = slot_store.shape[0]
    zeros_own = jnp.zeros((owner_width, row_count), jnp.bfloat16)
    full_first, full_second = (
        lax.all_gather(weight_first, "rep", axis=1, tiled=True),
        lax.all_gather(weight_second, "rep", axis=1, tiled=True),
    )
    first_tiles = order_tiles(full_first[0], links_first[0])
    second_tiles = order_tiles(full_second[0], links_second[0])
    handed = zeros_own
    tick_total = 2 * section_count - 1
    for tick_index in range(tick_total):
        if tick_index < section_count:
            incoming = jnp.where(section_here == 0, slot_store, handed)
        else:
            incoming = handed
        active = jnp.logical_and(
            section_here <= tick_index, section_here > tick_index - section_count
        )
        own_half = lax.all_to_all(incoming, "owners", split_axis=0, concat_axis=0, tiled=True)
        other_half = swapped(own_half, "owners", 0)
        lower_half = jnp.where(owner_parity == 0, own_half, other_half)
        upper_half = jnp.where(owner_parity == 0, other_half, own_half)
        apply_group_rows = jnp.concatenate([lower_half, upper_half], axis=0)
        middle = lax.cond(
            active,
            lambda: mixed_layer(apply_group_rows, first_tiles, bias_first[0]),
            lambda: zeros_own,
        )
        regrouped = lax.all_to_all(middle, "owners", split_axis=0, concat_axis=0, tiled=True)
        group_rows = regrouped
        result = lax.cond(
            active, lambda: mixed_layer(group_rows, second_tiles, bias_second[0]), lambda: zeros_own
        )
        if tick_index >= section_count - 1:
            slot_store = jnp.where(section_here == section_count - 1, result, slot_store)
        if tick_index < tick_total - 1:
            handed = passed_along(result, "section", 1)
        slot_store = rotate_slots(slot_store)
    slot_store = rotate_slots(slot_store)
    return slot_store[None]


def body(*arrays):
    inputs, weight_first = arrays[:2]
    owner_count = lax.axis_size("owners")
    size = weight_first.shape[3]
    width = inputs.shape[1]
    fits = (
        lax.axis_size("section") == 2
        and lax.axis_size("rep") == 2
        and owner_count == 4
        and width == 2 * size * owner_count
        and weight_first.shape[2] == 2 * width
        and arrays[2].shape[2] == width
    )
    return fast_body(*arrays) if fits else general_body(*arrays)


def solution(mesh):
    placed = (
        P("section", "owners", ("groups", "rep")),
        P("section", ("owners", "rep"), None, None),
        P("section", ("owners", "rep"), None, None),
        P("section", "owners"),
        P("section", "owners"),
        P("section", "owners", None),
        P("section", "owners", None),
    )
    return jax.shard_map(
        body,
        mesh=mesh,
        in_specs=placed,
        out_specs=P("section", "owners", ("groups", "rep")),
        check_vma=False,
    )
```

```python
import functools

import jax
import jax.numpy as jnp
from jax import lax
from jax.experimental import pallas as pl
from jax.experimental.pallas import tpu as pltpu
from jax.sharding import PartitionSpec as P

CEILING = 4.0


def order_kernel(links, own_tiles, other_tiles, bias, ordered, shifts):
    owner_count = ordered.shape[0]
    me, rep = lax.axis_index("owners"), lax.axis_index("rep")
    half, _, size = own_tiles.shape
    slots = links.shape[1]
    width = 2 * size
    for ours, source in ((True, own_tiles), (False, other_tiles)):
        first = (rep if ours else 1 - rep) * half
        for block in range(half):
            row = first + block
            distance = (row // 2) ^ me
            for slot in range(slots):
                place = links[row, slot]
                sender = ((place // 2) & (owner_count - 1)) ^ me
                if slots > 2 * owner_count:
                    part = (place // (2 * owner_count)) ^ (me & 1)
                    key = 2 * sender + part
                else:
                    key = sender
                low = pl.multiple_of(key * width + (place & 1) * size, size)
                ordered[distance, pl.ds(low, size), pl.ds(block % 2 * size, size)] = source[
                    block, pl.ds(slot * size, size), :
                ]
    for distance in range(owner_count):
        for j in range(2):
            shifts[pl.ds(distance, 1), pl.ds(j * size, size)] = bias[pl.ds(2 * (me ^ distance) + j, 1), :]


def order_weights(links, own_tiles, other_tiles, bias):
    half, depth, size = own_tiles.shape
    vmem = pl.BlockSpec(memory_space=pltpu.VMEM)
    return pl.pallas_call(
        order_kernel,
        out_shape=[
            jax.ShapeDtypeStruct((half, depth, 2 * size), jnp.bfloat16),
            jax.ShapeDtypeStruct((half, 2 * size), jnp.float32),
        ],
        in_specs=[pl.BlockSpec(memory_space=pltpu.SMEM), vmem, vmem, vmem],
        out_specs=[vmem, vmem],
        compiler_params=pltpu.CompilerParams(vmem_limit_bytes=24 * 2**20),
        cost_estimate=pl.CostEstimate(flops=1, bytes_accessed=1, transcendentals=0),
    )(links, own_tiles, other_tiles, bias)


def layer_kernel(tile_list, out_groups, raw, final, active_section, *refs):
    ordered, shifts = refs[:2]
    buffer_count = 1 + max(buffer for buffer, _, _ in tile_list)
    buffers = refs[2 : 2 + buffer_count]
    rest = list(refs[2 + buffer_count :])
    settled = rest.pop(0) if final == "merge" else None
    out_count = 1 if final else len(out_groups)
    outs = rest[:out_count]
    turned = rest[out_count] if raw else None
    section = lax.axis_index("section")
    me = lax.axis_index("owners")
    width = ordered.shape[2]

    def run():
        if raw:
            for place, (buffer, column, _) in enumerate(tile_list):
                turned[place] = buffers[buffer][pl.ds(column, width), :].T
        for distance in reversed(range(ordered.shape[0])):
            total = shifts[pl.ds(distance, 1), :]
            for place, (buffer, column, key) in enumerate(tile_list):
                left = turned[place] if raw else buffers[buffer][:, pl.ds(column, width)]
                if raw:
                    key = (key & ~1) + ((key & 1) ^ (me & 1))
                low = pl.multiple_of(key * width, width) if raw else key * width
                right = ordered[distance, pl.ds(low, width), :]
                total = total + jnp.dot(left, right, preferred_element_type=jnp.float32)
            value = jnp.clip(total, 0.0, CEILING).astype(jnp.bfloat16)
            if final:
                outs[0][pl.ds(pl.multiple_of((me ^ distance) * width, width), width), :] = value.T
            else:
                for out, group in zip(outs, out_groups, strict=True):
                    if distance in group:
                        out[:, pl.ds(group.index(distance) * width, width)] = value

    pl.when(section == active_section)(run)
    if final == "merge":

        @pl.when(section != active_section)
        def _():
            outs[0][...] = settled[...]


def layer(ordered, shifts, buffers, tile_list, out_groups, active_section, raw=False, final=None, settled=None):
    count, depth, width = ordered.shape
    rows = buffers[0].shape[1] if raw else buffers[0].shape[0]
    if final:
        shapes = [jax.ShapeDtypeStruct((count * width, rows), jnp.bfloat16)]
    else:
        shapes = [jax.ShapeDtypeStruct((rows, len(group) * width), jnp.bfloat16) for group in out_groups]
    vmem = pl.BlockSpec(memory_space=pltpu.VMEM)
    operands = [ordered, shifts, *buffers] + ([settled] if final == "merge" else [])
    return pl.pallas_call(
        functools.partial(layer_kernel, tile_list, out_groups, raw, final, active_section),
        out_shape=shapes,
        in_specs=[vmem] * len(operands),
        out_specs=[vmem] * len(shapes),
        scratch_shapes=[pltpu.VMEM((len(tile_list), rows, width), jnp.bfloat16)] if raw else [],
        compiler_params=pltpu.CompilerParams(vmem_limit_bytes=16 * 2**20),
        cost_estimate=pl.CostEstimate(flops=1, bytes_accessed=1, transcendentals=0),
    )(*operands)


def fast_body(inputs, weight_first, weight_second, bias_first, bias_second, links_first, links_second):
    owner_count = lax.axis_size("owners")
    me = lax.axis_index("owners")
    size = weight_first.shape[3]
    features = inputs[0]
    piece = features.shape[0] // owner_count

    def moved(value, distance, cross):
        pairs = []
        for owner in range(owner_count):
            for place in range(2):
                target = (owner ^ distance) * 2 + (1 - place if cross else place)
                pairs.append((owner * 2 + place, target))
        return lax.ppermute(value, ("owners", "section"), pairs)

    def other_core(value):
        return lax.ppermute(value, "rep", [(0, 1), (1, 0)])

    halves = features.reshape(2, 2 * piece, features.shape[1])
    near = lax.dynamic_index_in_dim(halves, me // 2, 0, keepdims=False)
    far = lax.dynamic_index_in_dim(halves, 1 - me // 2, 0, keepdims=False)
    three, two, one = moved(far, 3, False), moved(far, 2, False), moved(near, 1, False)
    start = [near, one, two, three]
    first_own, second_own = weight_first[0], weight_second[0]
    first = order_weights(links_first[0], first_own, other_core(first_own), bias_first[0].reshape(-1, size))
    second = order_weights(links_second[0], second_own, other_core(second_own), bias_second[0].reshape(-1, size))

    raw_tiles = [(buffer, column * piece, 2 * buffer + column) for buffer in range(4) for column in range(2)]
    relayed = [(0, 0), (0, 1), (1, 1), (1, 0), (2, 0), (3, 0), (3, 1), (2, 1)]
    relayed_spots = [(0, 0), (0, piece), (1, 0), (1, piece), (2, 0), (3, 0), (4, 0), (5, 0)]
    relayed_tiles = [
        (*spot, 2 * sender + part) for spot, (sender, part) in zip(relayed_spots, relayed, strict=True)
    ]
    second_tiles = [(buffer, 0, buffer) for buffer in range(4)]

    apart = [[0], [1], [2], [3]]
    joined = [[0, 1], [2], [3]]

    def first_layer(buffers, active, raw):
        return layer(*first, buffers, raw_tiles if raw else relayed_tiles, apart, active, raw=raw)

    def second_layer(parts, active, **more):
        arrived = [moved(parts[distance], distance, False) for distance in (3, 2, 1)]
        return layer(*second, [parts[0], *arrived[::-1]], second_tiles, joined, active, **more)

    def hand_over(result):
        close, far_two, far_three = result
        two, three = moved(far_two, 2, True), moved(far_three, 3, True)
        close = moved(close, 0, True)
        return [close, moved(close, 1, False), two, three, moved(two, 1, False), moved(three, 1, False)]

    later = [moved(value, 0, True) for value in start]
    zero = second_layer(first_layer(start, 0, True), 0)
    one = second_layer(first_layer(later, 0, True), 0)
    settled = second_layer(first_layer(hand_over(zero), 1, False), 1, final="plain")[0]
    settled = moved(settled, 0, True)
    return second_layer(first_layer(hand_over(one), 1, False), 1, final="merge", settled=settled)[0][None]


def from_behind(value, axis, steps):
    count = lax.axis_size(axis)
    pairs = [(source, (source + steps) % count) for source in range(count)]
    return lax.ppermute(value, axis, pairs)


def swapped(block, axis, distance):
    count = lax.axis_size(axis)
    route = []
    for low in range(count):
        high = low | 1 << distance
        if high != low and high < count:
            route += [(low, high), (high, low)]
    return lax.ppermute(block, axis, route)


def passed_along(array, axis, by):
    size = lax.axis_size(axis)
    pairs = [(i, i + by) for i in range(size) if 0 <= i + by < size]
    return lax.ppermute(array, axis, pairs)


def order_tiles(tiles, link_table):
    block_count = tiles.shape[0]
    radix_len = link_table.shape[1]
    tile_size = tiles.shape[2]
    inverse = jnp.argsort(link_table, axis=1)
    shaped = tiles.reshape(block_count, radix_len, tile_size, tile_size)
    ordered = jnp.take_along_axis(shaped, inverse[:, :, None, None], axis=1)
    return ordered.reshape(block_count, radix_len * tile_size, tile_size)


def mixed_layer(group_rows, ordered, bias_row):
    block_count = ordered.shape[0]
    tile_size = ordered.shape[2]
    row_count = group_rows.shape[1]
    summed = jnp.einsum("bkc,kr->bcr", ordered, group_rows, preferred_element_type=jnp.float32)
    summed = summed.reshape(block_count * tile_size, row_count) + bias_row[:, None]
    return jnp.clip(summed, 0.0, CEILING).astype(jnp.bfloat16)


def rotate_slots(slot_store):
    return from_behind(slot_store, "section", 1)


def general_body(inputs, weight_first, weight_second, bias_first, bias_second, links_first, links_second):
    section_count = lax.axis_size("section")
    section_here = lax.axis_index("section")
    owner_parity = lax.axis_index("owners") % 2
    slot_store = inputs[0]
    row_count = slot_store.shape[1]
    owner_width = slot_store.shape[0]
    zeros_own = jnp.zeros((owner_width, row_count), jnp.bfloat16)
    full_first, full_second = (
        lax.all_gather(weight_first, "rep", axis=1, tiled=True),
        lax.all_gather(weight_second, "rep", axis=1, tiled=True),
    )
    first_tiles = order_tiles(full_first[0], links_first[0])
    second_tiles = order_tiles(full_second[0], links_second[0])
    handed = zeros_own
    tick_total = 2 * section_count - 1
    for tick_index in range(tick_total):
        if tick_index < section_count:
            incoming = jnp.where(section_here == 0, slot_store, handed)
        else:
            incoming = handed
        active = jnp.logical_and(
            section_here <= tick_index, section_here > tick_index - section_count
        )
        own_half = lax.all_to_all(incoming, "owners", split_axis=0, concat_axis=0, tiled=True)
        other_half = swapped(own_half, "owners", 0)
        lower_half = jnp.where(owner_parity == 0, own_half, other_half)
        upper_half = jnp.where(owner_parity == 0, other_half, own_half)
        apply_group_rows = jnp.concatenate([lower_half, upper_half], axis=0)
        middle = lax.cond(
            active,
            lambda: mixed_layer(apply_group_rows, first_tiles, bias_first[0]),
            lambda: zeros_own,
        )
        regrouped = lax.all_to_all(middle, "owners", split_axis=0, concat_axis=0, tiled=True)
        group_rows = regrouped
        result = lax.cond(
            active, lambda: mixed_layer(group_rows, second_tiles, bias_second[0]), lambda: zeros_own
        )
        if tick_index >= section_count - 1:
            slot_store = jnp.where(section_here == section_count - 1, result, slot_store)
        if tick_index < tick_total - 1:
            handed = passed_along(result, "section", 1)
        slot_store = rotate_slots(slot_store)
    slot_store = rotate_slots(slot_store)
    return slot_store[None]


def body(*arrays):
    inputs, weight_first = arrays[:2]
    owner_count = lax.axis_size("owners")
    size = weight_first.shape[3]
    width = inputs.shape[1]
    fits = (
        lax.axis_size("section") == 2
        and lax.axis_size("rep") == 2
        and owner_count == 4
        and width == 2 * size * owner_count
        and weight_first.shape[2] == 2 * width
        and arrays[2].shape[2] == width
    )
    return fast_body(*arrays) if fits else general_body(*arrays)


def solution(mesh):
    placed = (
        P("section", "owners", ("groups", "rep")),
        P("section", ("owners", "rep"), None, None),
        P("section", ("owners", "rep"), None, None),
        P("section", "owners"),
        P("section", "owners"),
        P("section", "owners", None),
        P("section", "owners", None),
    )
    return jax.shard_map(
        body,
        mesh=mesh,
        in_specs=placed,
        out_specs=P("section", "owners", ("groups", "rep")),
        check_vma=False,
    )
```

```python
import functools

import jax
import jax.numpy as jnp
from jax import lax
from jax.experimental import pallas as pl
from jax.experimental.pallas import tpu as pltpu
from jax.sharding import PartitionSpec as P

CEILING = 4.0
LAG = 1
TAIL = 10**10


def order_kernel(links, own_tiles, other_tiles, bias, ordered, shifts, own_here, bias_here, arrivals):
    own_copy = pltpu.make_async_copy(own_tiles, own_here, arrivals.at[0])
    bias_copy = pltpu.make_async_copy(bias, bias_here, arrivals.at[1])
    own_copy.start()
    bias_copy.start()
    owner_count = ordered.shape[0]
    me, rep = lax.axis_index("owners"), lax.axis_index("rep")
    half, _, size = own_tiles.shape
    slots = links.shape[1]
    width = 2 * size
    for ours, source in ((False, other_tiles), (True, own_here)):
        if ours:
            own_copy.wait()
        first = (rep if ours else 1 - rep) * half
        for block in range(half):
            row = first + block
            distance = (row // 2) ^ me
            for slot in range(slots):
                place = links[row, slot]
                sender = ((place // 2) & (owner_count - 1)) ^ me
                if slots > 2 * owner_count:
                    part = (place // (2 * owner_count)) ^ (me & 1)
                    key = 2 * sender + part
                else:
                    key = sender
                low = pl.multiple_of(key * width + (place & 1) * size, size)
                ordered[distance, pl.ds(low, size), pl.ds(block % 2 * size, size)] = source[
                    block, pl.ds(slot * size, size), :
                ]
    bias_copy.wait()
    for distance in range(owner_count):
        for j in range(2):
            shifts[pl.ds(distance, 1), pl.ds(j * size, size)] = bias_here[pl.ds(2 * (me ^ distance) + j, 1), :]


def order_weights(links, own_tiles, other_tiles, bias):
    half, depth, size = own_tiles.shape
    vmem = pl.BlockSpec(memory_space=pltpu.VMEM)
    hbm = pl.BlockSpec(memory_space=pl.ANY)
    return pl.pallas_call(
        order_kernel,
        out_shape=[
            jax.ShapeDtypeStruct((half, depth, 2 * size), jnp.bfloat16),
            jax.ShapeDtypeStruct((half, 2 * size), jnp.float32),
        ],
        in_specs=[pl.BlockSpec(memory_space=pltpu.SMEM), hbm, vmem, hbm],
        out_specs=[vmem, vmem],
        scratch_shapes=[
            pltpu.VMEM(own_tiles.shape, jnp.bfloat16),
            pltpu.VMEM(bias.shape, jnp.float32),
            pltpu.SemaphoreType.DMA((2,)),
        ],
        compiler_params=pltpu.CompilerParams(vmem_limit_bytes=24 * 2**20),
        cost_estimate=pl.CostEstimate(flops=1, bytes_accessed=1, transcendentals=0),
    )(links, own_tiles, other_tiles, bias)


def layer_kernel(tile_list, out_groups, raw, final, active_section, *refs):
    ordered, shifts = refs[:2]
    buffer_count = 1 + max(buffer for buffer, _, _ in tile_list)
    buffers = refs[2 : 2 + buffer_count]
    rest = list(refs[2 + buffer_count :])
    settled = rest.pop(0) if final == "merge" else None
    out_count = 1 if final else len(out_groups)
    outs = rest[:out_count]
    turned = rest[out_count] if raw else None
    section = lax.axis_index("section")
    me = lax.axis_index("owners")
    width = ordered.shape[2]

    def run():
        if raw:
            for place, (buffer, column, _) in enumerate(tile_list):
                turned[place] = buffers[buffer][pl.ds(column, width), :].T
        for distance in reversed(range(ordered.shape[0])):
            total = shifts[pl.ds(distance, 1), :]
            for place, (buffer, column, key) in enumerate(tile_list):
                left = turned[place] if raw else buffers[buffer][:, pl.ds(column, width)]
                if raw:
                    key = (key & ~1) + ((key & 1) ^ (me & 1))
                low = pl.multiple_of(key * width, width) if raw else key * width
                right = ordered[distance, pl.ds(low, width), :]
                total = total + jnp.dot(left, right, preferred_element_type=jnp.float32)
            value = jnp.clip(total, 0.0, CEILING).astype(jnp.bfloat16)
            if final:
                outs[0][pl.ds(pl.multiple_of((me ^ distance) * width, width), width), :] = value.T
            else:
                for out, group in zip(outs, out_groups, strict=True):
                    if distance in group:
                        out[:, pl.ds(group.index(distance) * width, width)] = value

    pl.when(section == active_section)(run)
    if final == "merge":

        @pl.when(section != active_section)
        def _():
            outs[0][...] = settled[...]


def layer(ordered, shifts, buffers, tile_list, out_groups, active_section, raw=False, final=None, settled=None, cost=1):
    count, depth, width = ordered.shape
    rows = buffers[0].shape[1] if raw else buffers[0].shape[0]
    if final:
        shapes = [jax.ShapeDtypeStruct((count * width, rows), jnp.bfloat16)]
    else:
        shapes = [jax.ShapeDtypeStruct((rows, len(group) * width), jnp.bfloat16) for group in out_groups]
    vmem = pl.BlockSpec(memory_space=pltpu.VMEM)
    operands = [ordered, shifts, *buffers] + ([settled] if final == "merge" else [])
    return pl.pallas_call(
        functools.partial(layer_kernel, tile_list, out_groups, raw, final, active_section),
        out_shape=shapes,
        in_specs=[vmem] * len(operands),
        out_specs=[vmem] * len(shapes),
        scratch_shapes=[pltpu.VMEM((len(tile_list), rows, width), jnp.bfloat16)] if raw else [],
        compiler_params=pltpu.CompilerParams(vmem_limit_bytes=16 * 2**20),
        cost_estimate=pl.CostEstimate(flops=cost, bytes_accessed=1, transcendentals=0),
    )(*operands)


def fast_body(inputs, weight_first, weight_second, bias_first, bias_second, links_first, links_second):
    owner_count = lax.axis_size("owners")
    me = lax.axis_index("owners")
    size = weight_first.shape[3]
    features = inputs[0]
    piece = features.shape[0] // owner_count

    def moved(value, route):
        pairs = []
        for owner in range(owner_count):
            for place in range(2):
                for core in range(2):
                    to_owner, to_place, to_core = route(owner, place, core)
                    pairs.append(((owner * 2 + place) * 2 + core, (to_owner * 2 + to_place) * 2 + to_core))
        return lax.ppermute(value, ("owners", "section", "rep"), pairs)

    def within(distance, section):
        return lambda owner, place, core: (owner ^ distance, place, core) if place == section else (owner, place, 1 - core)

    def across(distance, section):
        return lambda owner, place, core: (owner ^ distance if place == section else owner, 1 - place, core)

    def other_core(value):
        return lax.ppermute(value, "rep", [(0, 1), (1, 0)])

    halves = features.reshape(2, 2 * piece, features.shape[1])
    near = lax.dynamic_index_in_dim(halves, me // 2, 0, keepdims=False)
    far = lax.dynamic_index_in_dim(halves, 1 - me // 2, 0, keepdims=False)
    def after(value, *others):
        return lax.optimization_barrier((value, *others))[0]

    def gathered(close, apart, section):
        beside = within(1, section)
        return [close, moved(close, beside), apart, moved(apart, beside)]

    first_own, second_own = weight_first[0], weight_second[0]
    first_other = other_core(first_own)
    far_two, near_one = moved(far, within(2, 0)), moved(near, within(1, 0))
    crossed = moved(far, across(2, 1)), moved(near, across(0, 1))
    first = order_weights(links_first[0], first_own, first_other, bias_first[0].reshape(-1, size))
    second_other = other_core(second_own)
    second = order_weights(links_second[0], second_own, second_other, bias_second[0].reshape(-1, size))
    start = [near, near_one, far_two, moved(after(far_two, first[0]), within(1, 0))]
    later = gathered(crossed[1], crossed[0], 0)

    raw_tiles = [(buffer, column * piece, 2 * buffer + column) for buffer in range(4) for column in range(2)]
    order = [(0, 0), (0, 1), (1, 1), (1, 0), (2, 0), (2, 1), (3, 1), (3, 0)]
    later_tiles = [(place // 2, place % 2 * piece, 2 * sender + part) for place, (sender, part) in enumerate(order)]
    second_tiles = [(buffer, 0, buffer) for buffer in range(4)]

    apart = [[0], [1], [2], [3]]
    joined = [[0, 1], [2, 3]]

    def first_layer(buffers, active, raw, cost=1):
        spots = raw_tiles if raw else later_tiles
        return layer(*first, buffers, spots, apart, active, raw=raw, cost=cost)

    def second_layer(parts, active, earlier, **more):
        arrived = [moved(parts[distance], within(distance, active)) for distance in (3, 2, 1)]
        buffers = after([parts[0], *arrived[::-1]], earlier)
        return layer(*second, buffers, second_tiles, joined, active, **more)

    def hand_over(result):
        close, apart = result
        return gathered(moved(close, across(0, 0)), moved(apart, across(2, 0)), 1)

    parts_zero = first_layer(start, 0, True, cost=LAG)
    parts_one = first_layer(after(later, parts_zero), 0, True)
    zero = second_layer(parts_zero, 0, parts_one, cost=LAG)
    one = second_layer(parts_one, 0, zero)
    parts_zero = first_layer(after(hand_over(zero), one), 1, False, cost=LAG)
    parts_one = first_layer(after(hand_over(one), parts_zero), 1, False)
    settled = second_layer(parts_zero, 1, parts_one, final="plain", cost=LAG)
    last = second_layer(parts_one, 1, settled, final="plain", cost=TAIL)[0]
    return jnp.where(lax.axis_index("section") == 0, moved(settled[0], across(0, 1)), last)[None]


def from_behind(value, axis, steps):
    count = lax.axis_size(axis)
    pairs = [(source, (source + steps) % count) for source in range(count)]
    return lax.ppermute(value, axis, pairs)


def swapped(block, axis, distance):
    count = lax.axis_size(axis)
    route = []
    for low in range(count):
        high = low | 1 << distance
        if high != low and high < count:
            route += [(low, high), (high, low)]
    return lax.ppermute(block, axis, route)


def passed_along(array, axis, by):
    size = lax.axis_size(axis)
    pairs = [(i, i + by) for i in range(size) if 0 <= i + by < size]
    return lax.ppermute(array, axis, pairs)


def order_tiles(tiles, link_table):
    block_count = tiles.shape[0]
    radix_len = link_table.shape[1]
    tile_size = tiles.shape[2]
    inverse = jnp.argsort(link_table, axis=1)
    shaped = tiles.reshape(block_count, radix_len, tile_size, tile_size)
    ordered = jnp.take_along_axis(shaped, inverse[:, :, None, None], axis=1)
    return ordered.reshape(block_count, radix_len * tile_size, tile_size)


def mixed_layer(group_rows, ordered, bias_row):
    block_count = ordered.shape[0]
    tile_size = ordered.shape[2]
    row_count = group_rows.shape[1]
    summed = jnp.einsum("bkc,kr->bcr", ordered, group_rows, preferred_element_type=jnp.float32)
    summed = summed.reshape(block_count * tile_size, row_count) + bias_row[:, None]
    return jnp.clip(summed, 0.0, CEILING).astype(jnp.bfloat16)


def rotate_slots(slot_store):
    return from_behind(slot_store, "section", 1)


def general_body(inputs, weight_first, weight_second, bias_first, bias_second, links_first, links_second):
    section_count = lax.axis_size("section")
    section_here = lax.axis_index("section")
    owner_parity = lax.axis_index("owners") % 2
    slot_store = inputs[0]
    row_count = slot_store.shape[1]
    owner_width = slot_store.shape[0]
    zeros_own = jnp.zeros((owner_width, row_count), jnp.bfloat16)
    full_first, full_second = (
        lax.all_gather(weight_first, "rep", axis=1, tiled=True),
        lax.all_gather(weight_second, "rep", axis=1, tiled=True),
    )
    first_tiles = order_tiles(full_first[0], links_first[0])
    second_tiles = order_tiles(full_second[0], links_second[0])
    handed = zeros_own
    tick_total = 2 * section_count - 1
    for tick_index in range(tick_total):
        if tick_index < section_count:
            incoming = jnp.where(section_here == 0, slot_store, handed)
        else:
            incoming = handed
        active = jnp.logical_and(
            section_here <= tick_index, section_here > tick_index - section_count
        )
        own_half = lax.all_to_all(incoming, "owners", split_axis=0, concat_axis=0, tiled=True)
        other_half = swapped(own_half, "owners", 0)
        lower_half = jnp.where(owner_parity == 0, own_half, other_half)
        upper_half = jnp.where(owner_parity == 0, other_half, own_half)
        apply_group_rows = jnp.concatenate([lower_half, upper_half], axis=0)
        middle = lax.cond(
            active,
            lambda: mixed_layer(apply_group_rows, first_tiles, bias_first[0]),
            lambda: zeros_own,
        )
        regrouped = lax.all_to_all(middle, "owners", split_axis=0, concat_axis=0, tiled=True)
        group_rows = regrouped
        result = lax.cond(
            active, lambda: mixed_layer(group_rows, second_tiles, bias_second[0]), lambda: zeros_own
        )
        if tick_index >= section_count - 1:
            slot_store = jnp.where(section_here == section_count - 1, result, slot_store)
        if tick_index < tick_total - 1:
            handed = passed_along(result, "section", 1)
        slot_store = rotate_slots(slot_store)
    slot_store = rotate_slots(slot_store)
    return slot_store[None]


def body(*arrays):
    inputs, weight_first = arrays[:2]
    owner_count = lax.axis_size("owners")
    size = weight_first.shape[3]
    width = inputs.shape[1]
    fits = (
        lax.axis_size("section") == 2
        and lax.axis_size("rep") == 2
        and owner_count == 4
        and width == 2 * size * owner_count
        and weight_first.shape[2] == 2 * width
        and arrays[2].shape[2] == width
    )
    return fast_body(*arrays) if fits else general_body(*arrays)


def solution(mesh):
    placed = (
        P("section", "owners", ("groups", "rep")),
        P("section", ("owners", "rep"), None, None),
        P("section", ("owners", "rep"), None, None),
        P("section", "owners"),
        P("section", "owners"),
        P("section", "owners", None),
        P("section", "owners", None),
    )
    return jax.shard_map(
        body,
        mesh=mesh,
        in_specs=placed,
        out_specs=P("section", "owners", ("groups", "rep")),
        check_vma=False,
    )
```

```python
import functools

import jax
import jax.numpy as jnp
from jax import lax
from jax.experimental import pallas as pl
from jax.experimental.pallas import tpu as pltpu
from jax.sharding import PartitionSpec as P

CEILING = 4.0
LAG = 1
TAIL = 10**10


def place_tiles(links, source, ordered, first):
    owner_count = ordered.shape[0]
    me = lax.axis_index("owners")
    half, _, size = source.shape
    slots = links.shape[1]
    width = 2 * size
    for block in range(half):
        row = first + block
        distance = (row // 2) ^ me
        for slot in range(slots):
            place = links[row, slot]
            sender = ((place // 2) & (owner_count - 1)) ^ me
            if slots > 2 * owner_count:
                part = (place // (2 * owner_count)) ^ (me & 1)
                key = 2 * sender + part
            else:
                key = sender
            low = pl.multiple_of(key * width + (place & 1) * size, size)
            ordered[distance, pl.ds(low, size), pl.ds(block % 2 * size, size)] = source[
                block, pl.ds(slot * size, size), :
            ]


def order_other_kernel(links, other_tiles, ordered):
    place_tiles(links, other_tiles, ordered, (1 - lax.axis_index("rep")) * other_tiles.shape[0])


def order_own_kernel(links, own_tiles, bias, half_ordered, ordered, shifts):
    place_tiles(links, own_tiles, ordered, lax.axis_index("rep") * own_tiles.shape[0])
    size = own_tiles.shape[2]
    for distance in range(shifts.shape[0]):
        for j in range(2):
            row = 2 * (lax.axis_index("owners") ^ distance) + j
            shifts[pl.ds(distance, 1), pl.ds(j * size, size)] = bias[pl.ds(row, 1), :]


def order_weights(links, own_tiles, other_tiles, bias):
    half, depth, size = own_tiles.shape
    vmem = pl.BlockSpec(memory_space=pltpu.VMEM)
    smem = pl.BlockSpec(memory_space=pltpu.SMEM)
    ordered = jax.ShapeDtypeStruct((half, depth, 2 * size), jnp.bfloat16)
    common = dict(
        compiler_params=pltpu.CompilerParams(vmem_limit_bytes=24 * 2**20),
        cost_estimate=pl.CostEstimate(flops=1, bytes_accessed=1, transcendentals=0),
    )
    half_ordered = pl.pallas_call(
        order_other_kernel, out_shape=ordered, in_specs=[smem, vmem], out_specs=vmem, **common
    )(links, other_tiles)
    return pl.pallas_call(
        order_own_kernel,
        out_shape=[ordered, jax.ShapeDtypeStruct((half, 2 * size), jnp.float32)],
        in_specs=[smem, vmem, vmem, vmem],
        out_specs=[vmem, vmem],
        input_output_aliases={3: 0},
        **common,
    )(links, own_tiles, bias, half_ordered)


def layer_kernel(tile_list, out_groups, raw, final, active_section, *refs):
    ordered, shifts = refs[:2]
    buffer_count = 1 + max(buffer for buffer, _, _ in tile_list)
    buffers = refs[2 : 2 + buffer_count]
    rest = list(refs[2 + buffer_count :])
    settled = rest.pop(0) if final == "merge" else None
    out_count = 1 if final else len(out_groups)
    outs = rest[:out_count]
    turned = rest[out_count] if raw else None
    section = lax.axis_index("section")
    me = lax.axis_index("owners")
    width = ordered.shape[2]

    def run():
        if raw:
            for place, (buffer, column, _) in enumerate(tile_list):
                turned[place] = buffers[buffer][pl.ds(column, width), :].T
        for distance in reversed(range(ordered.shape[0])):
            total = shifts[pl.ds(distance, 1), :]
            for place, (buffer, column, key) in enumerate(tile_list):
                left = turned[place] if raw else buffers[buffer][:, pl.ds(column, width)]
                if raw:
                    key = (key & ~1) + ((key & 1) ^ (me & 1))
                low = pl.multiple_of(key * width, width) if raw else key * width
                right = ordered[distance, pl.ds(low, width), :]
                total = total + jnp.dot(left, right, preferred_element_type=jnp.float32)
            value = jnp.clip(total, 0.0, CEILING).astype(jnp.bfloat16)
            if final:
                outs[0][pl.ds(pl.multiple_of((me ^ distance) * width, width), width), :] = value.T
            else:
                for out, group in zip(outs, out_groups, strict=True):
                    if distance in group:
                        out[:, pl.ds(group.index(distance) * width, width)] = value

    pl.when(section == active_section)(run)
    if final == "merge":

        @pl.when(section != active_section)
        def _():
            outs[0][...] = settled[...]


def layer(ordered, shifts, buffers, tile_list, out_groups, active_section, raw=False, final=None, settled=None, cost=1):
    count, depth, width = ordered.shape
    rows = buffers[0].shape[1] if raw else buffers[0].shape[0]
    if final:
        shapes = [jax.ShapeDtypeStruct((count * width, rows), jnp.bfloat16)]
    else:
        shapes = [jax.ShapeDtypeStruct((rows, len(group) * width), jnp.bfloat16) for group in out_groups]
    vmem = pl.BlockSpec(memory_space=pltpu.VMEM)
    operands = [ordered, shifts, *buffers] + ([settled] if final == "merge" else [])
    return pl.pallas_call(
        functools.partial(layer_kernel, tile_list, out_groups, raw, final, active_section),
        out_shape=shapes,
        in_specs=[vmem] * len(operands),
        out_specs=[vmem] * len(shapes),
        scratch_shapes=[pltpu.VMEM((len(tile_list), rows, width), jnp.bfloat16)] if raw else [],
        compiler_params=pltpu.CompilerParams(vmem_limit_bytes=16 * 2**20),
        cost_estimate=pl.CostEstimate(flops=cost, bytes_accessed=1, transcendentals=0),
    )(*operands)


def fast_body(inputs, weight_first, weight_second, bias_first, bias_second, links_first, links_second):
    owner_count = lax.axis_size("owners")
    me = lax.axis_index("owners")
    size = weight_first.shape[3]
    features = inputs[0]
    piece = features.shape[0] // owner_count

    def moved(value, route):
        pairs = []
        for owner in range(owner_count):
            for place in range(2):
                for core in range(2):
                    to_owner, to_place, to_core = route(owner, place, core)
                    pairs.append(((owner * 2 + place) * 2 + core, (to_owner * 2 + to_place) * 2 + to_core))
        return lax.ppermute(value, ("owners", "section", "rep"), pairs)

    def within(distance, section):
        return lambda owner, place, core: (owner ^ distance, place, core) if place == section else (owner, place, 1 - core)

    def across(distance, section):
        return lambda owner, place, core: (owner ^ distance if place == section else owner, 1 - place, 1 - core)

    def other_core(value):
        return lax.ppermute(value, "rep", [(0, 1), (1, 0)])

    halves = features.reshape(2, 2 * piece, features.shape[1])
    near = lax.dynamic_index_in_dim(halves, me // 2, 0, keepdims=False)
    far = lax.dynamic_index_in_dim(halves, 1 - me // 2, 0, keepdims=False)
    def after(value, *others):
        return lax.optimization_barrier((value, *others))[0]

    def gathered(close, apart, section):
        beside = within(1, section)
        return [close, moved(close, beside), apart, moved(apart, beside)]

    first_own, second_own = weight_first[0], weight_second[0]
    first_other = other_core(first_own)
    far_two, near_one = moved(far, within(2, 0)), moved(near, within(1, 0))
    crossed = moved(far, across(2, 1)), moved(near, across(0, 1))
    first = order_weights(links_first[0], first_own, first_other, bias_first[0].reshape(-1, size))
    second_other = other_core(second_own)
    second = order_weights(links_second[0], second_own, second_other, bias_second[0].reshape(-1, size))
    start = [near, near_one, far_two, moved(after(far_two, first[0]), within(1, 0))]
    later = gathered(crossed[1], crossed[0], 0)

    raw_tiles = [(buffer, column * piece, 2 * buffer + column) for buffer in range(4) for column in range(2)]
    order = [(0, 0), (0, 1), (1, 1), (1, 0), (2, 0), (2, 1), (3, 1), (3, 0)]
    later_tiles = [(place // 2, place % 2 * piece, 2 * sender + part) for place, (sender, part) in enumerate(order)]
    second_tiles = [(buffer, 0, buffer) for buffer in range(4)]

    apart = [[0], [1], [2], [3]]
    joined = [[0, 1], [2, 3]]

    def first_layer(buffers, active, raw, cost=1):
        spots = raw_tiles if raw else later_tiles
        return layer(*first, buffers, spots, apart, active, raw=raw, cost=cost)

    def second_layer(parts, active, earlier, **more):
        arrived = {distance: moved(parts[distance], within(distance, active)) for distance in (2, 1, 3)}
        buffers = after([parts[0]] + [arrived[distance] for distance in range(1, owner_count)], earlier)
        return layer(*second, buffers, second_tiles, joined, active, **more)

    def hand_over(result):
        close, apart = result
        return gathered(moved(close, across(0, 0)), moved(apart, across(2, 0)), 1)

    parts_zero = first_layer(after(start, second[0]), 0, True, cost=LAG)
    parts_one = first_layer(after(later, parts_zero), 0, True)
    zero = second_layer(parts_zero, 0, parts_one, cost=LAG)
    one = second_layer(parts_one, 0, zero)
    parts_zero = first_layer(after(hand_over(zero), one), 1, False, cost=LAG)
    parts_one = first_layer(after(hand_over(one), parts_zero), 1, False)
    settled = second_layer(parts_zero, 1, parts_one, final="plain", cost=LAG)
    last = second_layer(parts_one, 1, settled, final="plain", cost=TAIL)[0]
    return jnp.where(lax.axis_index("section") == 0, moved(settled[0], across(0, 1)), last)[None]


def from_behind(value, axis, steps):
    count = lax.axis_size(axis)
    pairs = [(source, (source + steps) % count) for source in range(count)]
    return lax.ppermute(value, axis, pairs)


def swapped(block, axis, distance):
    count = lax.axis_size(axis)
    route = []
    for low in range(count):
        high = low | 1 << distance
        if high != low and high < count:
            route += [(low, high), (high, low)]
    return lax.ppermute(block, axis, route)


def passed_along(array, axis, by):
    size = lax.axis_size(axis)
    pairs = [(i, i + by) for i in range(size) if 0 <= i + by < size]
    return lax.ppermute(array, axis, pairs)


def order_tiles(tiles, link_table):
    block_count = tiles.shape[0]
    radix_len = link_table.shape[1]
    tile_size = tiles.shape[2]
    inverse = jnp.argsort(link_table, axis=1)
    shaped = tiles.reshape(block_count, radix_len, tile_size, tile_size)
    ordered = jnp.take_along_axis(shaped, inverse[:, :, None, None], axis=1)
    return ordered.reshape(block_count, radix_len * tile_size, tile_size)


def mixed_layer(group_rows, ordered, bias_row):
    block_count = ordered.shape[0]
    tile_size = ordered.shape[2]
    row_count = group_rows.shape[1]
    summed = jnp.einsum("bkc,kr->bcr", ordered, group_rows, preferred_element_type=jnp.float32)
    summed = summed.reshape(block_count * tile_size, row_count) + bias_row[:, None]
    return jnp.clip(summed, 0.0, CEILING).astype(jnp.bfloat16)


def rotate_slots(slot_store):
    return from_behind(slot_store, "section", 1)


def general_body(inputs, weight_first, weight_second, bias_first, bias_second, links_first, links_second):
    section_count = lax.axis_size("section")
    section_here = lax.axis_index("section")
    owner_parity = lax.axis_index("owners") % 2
    slot_store = inputs[0]
    row_count = slot_store.shape[1]
    owner_width = slot_store.shape[0]
    zeros_own = jnp.zeros((owner_width, row_count), jnp.bfloat16)
    full_first, full_second = (
        lax.all_gather(weight_first, "rep", axis=1, tiled=True),
        lax.all_gather(weight_second, "rep", axis=1, tiled=True),
    )
    first_tiles = order_tiles(full_first[0], links_first[0])
    second_tiles = order_tiles(full_second[0], links_second[0])
    handed = zeros_own
    tick_total = 2 * section_count - 1
    for tick_index in range(tick_total):
        if tick_index < section_count:
            incoming = jnp.where(section_here == 0, slot_store, handed)
        else:
            incoming = handed
        active = jnp.logical_and(
            section_here <= tick_index, section_here > tick_index - section_count
        )
        own_half = lax.all_to_all(incoming, "owners", split_axis=0, concat_axis=0, tiled=True)
        other_half = swapped(own_half, "owners", 0)
        lower_half = jnp.where(owner_parity == 0, own_half, other_half)
        upper_half = jnp.where(owner_parity == 0, other_half, own_half)
        apply_group_rows = jnp.concatenate([lower_half, upper_half], axis=0)
        middle = lax.cond(
            active,
            lambda: mixed_layer(apply_group_rows, first_tiles, bias_first[0]),
            lambda: zeros_own,
        )
        regrouped = lax.all_to_all(middle, "owners", split_axis=0, concat_axis=0, tiled=True)
        group_rows = regrouped
        result = lax.cond(
            active, lambda: mixed_layer(group_rows, second_tiles, bias_second[0]), lambda: zeros_own
        )
        if tick_index >= section_count - 1:
            slot_store = jnp.where(section_here == section_count - 1, result, slot_store)
        if tick_index < tick_total - 1:
            handed = passed_along(result, "section", 1)
        slot_store = rotate_slots(slot_store)
    slot_store = rotate_slots(slot_store)
    return slot_store[None]


def body(*arrays):
    inputs, weight_first = arrays[:2]
    owner_count = lax.axis_size("owners")
    size = weight_first.shape[3]
    width = inputs.shape[1]
    fits = (
        lax.axis_size("section") == 2
        and lax.axis_size("rep") == 2
        and owner_count == 4
        and width == 2 * size * owner_count
        and weight_first.shape[2] == 2 * width
        and arrays[2].shape[2] == width
    )
    return fast_body(*arrays) if fits else general_body(*arrays)


def solution(mesh):
    placed = (
        P("section", "owners", ("groups", "rep")),
        P("section", ("owners", "rep"), None, None),
        P("section", ("owners", "rep"), None, None),
        P("section", "owners"),
        P("section", "owners"),
        P("section", "owners", None),
        P("section", "owners", None),
    )
    return jax.shard_map(
        body,
        mesh=mesh,
        in_specs=placed,
        out_specs=P("section", "owners", ("groups", "rep")),
        check_vma=False,
    )
```

```python
import functools

import jax
import jax.numpy as jnp
from jax import lax
from jax.experimental import pallas as pl
from jax.experimental.pallas import tpu as pltpu
from jax.sharding import PartitionSpec as P

CEILING = 4.0
LAG = 1
TAIL = 10**10


def place_tiles(links, source, ordered, first):
    owner_count = ordered.shape[0]
    owner_bits = owner_count.bit_length() - 1
    me = lax.axis_index("owners")
    half, _, size = source.shape
    slots = links.shape[1]
    two_parts = slots > 2 * owner_count
    flip = me * 4 + (me & 1) * 2 if two_parts else me * 2
    for block in range(half):
        row = first + block
        distance = (row >> 1) ^ me
        for slot in range(slots):
            place = links[row, slot]
            if two_parts:
                key = ((place & (2 * owner_count - 2)) << 1) | ((place >> (owner_bits + 1)) << 1) | (place & 1)
            else:
                key = place
            low = pl.multiple_of((key ^ flip) * size, size)
            ordered[distance, pl.ds(low, size), pl.ds(block % 2 * size, size)] = source[
                block, pl.ds(slot * size, size), :
            ]


def order_other_kernel(links, other_tiles, ordered):
    place_tiles(links, other_tiles, ordered, (1 - lax.axis_index("rep")) * other_tiles.shape[0])


def order_own_kernel(links, own_tiles, bias, half_ordered, ordered, shifts):
    place_tiles(links, own_tiles, ordered, lax.axis_index("rep") * own_tiles.shape[0])
    size = own_tiles.shape[2]
    for distance in range(shifts.shape[0]):
        for j in range(2):
            row = 2 * (lax.axis_index("owners") ^ distance) + j
            shifts[pl.ds(distance, 1), pl.ds(j * size, size)] = bias[pl.ds(row, 1), :]


def order_weights(links, own_tiles, other_tiles, bias):
    half, depth, size = own_tiles.shape
    vmem = pl.BlockSpec(memory_space=pltpu.VMEM)
    smem = pl.BlockSpec(memory_space=pltpu.SMEM)
    ordered = jax.ShapeDtypeStruct((half, depth, 2 * size), jnp.bfloat16)
    common = dict(
        compiler_params=pltpu.CompilerParams(vmem_limit_bytes=24 * 2**20),
        cost_estimate=pl.CostEstimate(flops=1, bytes_accessed=1, transcendentals=0),
    )
    half_ordered = pl.pallas_call(
        order_other_kernel, out_shape=ordered, in_specs=[smem, vmem], out_specs=vmem, **common
    )(links, other_tiles)
    return pl.pallas_call(
        order_own_kernel,
        out_shape=[ordered, jax.ShapeDtypeStruct((half, 2 * size), jnp.float32)],
        in_specs=[smem, vmem, vmem, vmem],
        out_specs=[vmem, vmem],
        input_output_aliases={3: 0},
        **common,
    )(links, own_tiles, bias, half_ordered)


def layer_kernel(tile_list, out_groups, raw, final, active_section, *refs):
    ordered, shifts = refs[:2]
    buffer_count = 1 + max(buffer for buffer, _, _ in tile_list)
    buffers = refs[2 : 2 + buffer_count]
    rest = list(refs[2 + buffer_count :])
    settled = rest.pop(0) if final == "merge" else None
    out_count = 1 if final else len(out_groups)
    outs = rest[:out_count]
    turned = rest[out_count] if raw else None
    section = lax.axis_index("section")
    me = lax.axis_index("owners")
    width = ordered.shape[2]

    def run():
        if raw:
            for place, (buffer, column, _) in enumerate(tile_list):
                turned[place] = buffers[buffer][pl.ds(column, width), :].T
        for distance in reversed(range(ordered.shape[0])):
            total = shifts[pl.ds(distance, 1), :]
            for place, (buffer, column, key) in enumerate(tile_list):
                left = turned[place] if raw else buffers[buffer][:, pl.ds(column, width)]
                if raw:
                    key = (key & ~1) + ((key & 1) ^ (me & 1))
                low = pl.multiple_of(key * width, width) if raw else key * width
                right = ordered[distance, pl.ds(low, width), :]
                total = total + jnp.dot(left, right, preferred_element_type=jnp.float32)
            value = jnp.clip(total, 0.0, CEILING).astype(jnp.bfloat16)
            if final:
                outs[0][pl.ds(pl.multiple_of((me ^ distance) * width, width), width), :] = value.T
            else:
                for out, group in zip(outs, out_groups, strict=True):
                    if distance in group:
                        out[:, pl.ds(group.index(distance) * width, width)] = value

    pl.when(section == active_section)(run)
    if final == "merge":

        @pl.when(section != active_section)
        def _():
            outs[0][...] = settled[...]


def layer(ordered, shifts, buffers, tile_list, out_groups, active_section, raw=False, final=None, settled=None, cost=1):
    count, depth, width = ordered.shape
    rows = buffers[0].shape[1] if raw else buffers[0].shape[0]
    if final:
        shapes = [jax.ShapeDtypeStruct((count * width, rows), jnp.bfloat16)]
    else:
        shapes = [jax.ShapeDtypeStruct((rows, len(group) * width), jnp.bfloat16) for group in out_groups]
    vmem = pl.BlockSpec(memory_space=pltpu.VMEM)
    operands = [ordered, shifts, *buffers] + ([settled] if final == "merge" else [])
    return pl.pallas_call(
        functools.partial(layer_kernel, tile_list, out_groups, raw, final, active_section),
        out_shape=shapes,
        in_specs=[vmem] * len(operands),
        out_specs=[vmem] * len(shapes),
        scratch_shapes=[pltpu.VMEM((len(tile_list), rows, width), jnp.bfloat16)] if raw else [],
        compiler_params=pltpu.CompilerParams(vmem_limit_bytes=16 * 2**20),
        cost_estimate=pl.CostEstimate(flops=cost, bytes_accessed=1, transcendentals=0),
    )(*operands)


def fast_body(inputs, weight_first, weight_second, bias_first, bias_second, links_first, links_second):
    owner_count = lax.axis_size("owners")
    me = lax.axis_index("owners")
    size = weight_first.shape[3]
    features = inputs[0]
    piece = features.shape[0] // owner_count

    def moved(value, route):
        pairs = []
        for owner in range(owner_count):
            for place in range(2):
                for core in range(2):
                    to_owner, to_place, to_core = route(owner, place, core)
                    pairs.append(((owner * 2 + place) * 2 + core, (to_owner * 2 + to_place) * 2 + to_core))
        return lax.ppermute(value, ("owners", "section", "rep"), pairs)

    def within(distance, section):
        return lambda owner, place, core: (owner ^ distance, place, core) if place == section else (owner, place, 1 - core)

    def across(distance, section):
        return lambda owner, place, core: (owner ^ distance if place == section else owner, 1 - place, 1 - core)

    def other_core(value):
        return lax.ppermute(value, "rep", [(0, 1), (1, 0)])

    halves = features.reshape(2, 2 * piece, features.shape[1])
    near = lax.dynamic_index_in_dim(halves, me // 2, 0, keepdims=False)
    far = lax.dynamic_index_in_dim(halves, 1 - me // 2, 0, keepdims=False)
    def after(value, *others):
        return lax.optimization_barrier((value, *others))[0]

    def gathered(close, apart, section):
        beside = within(1, section)
        return [close, moved(close, beside), apart, moved(apart, beside)]

    first_own, second_own = weight_first[0], weight_second[0]
    first_other = other_core(first_own)
    far_two, near_one = moved(far, within(2, 0)), moved(near, within(1, 0))
    crossed_far = moved(far, across(2, 1))
    crossed_near = [moved(near, across(distance, 1)) for distance in (0, 1)]
    first = order_weights(links_first[0], first_own, first_other, bias_first[0].reshape(-1, size))
    second_other = other_core(second_own)
    second = order_weights(links_second[0], second_own, second_other, bias_second[0].reshape(-1, size))
    start = [near, near_one, far_two, moved(after(far_two, first[0]), within(1, 0))]
    later = [*crossed_near, crossed_far, moved(after(crossed_far, second[0]), within(1, 0))]

    raw_tiles = [(buffer, column * piece, 2 * buffer + column) for buffer in range(4) for column in range(2)]
    order = [(0, 0), (0, 1), (1, 1), (1, 0), (2, 0), (2, 1), (3, 1), (3, 0)]
    later_tiles = [(place // 2, place % 2 * piece, 2 * sender + part) for place, (sender, part) in enumerate(order)]
    second_tiles = [(buffer, 0, buffer) for buffer in range(4)]

    apart = [[0], [1], [2], [3]]
    joined = [[0, 1], [2, 3]]

    def first_layer(buffers, active, raw, cost=1):
        spots = raw_tiles if raw else later_tiles
        return layer(*first, buffers, spots, apart, active, raw=raw, cost=cost)

    def second_layer(parts, active, earlier, **more):
        arrived = {distance: moved(parts[distance], within(distance, active)) for distance in (2, 1, 3)}
        buffers = after([parts[0]] + [arrived[distance] for distance in range(1, owner_count)], earlier)
        return layer(*second, buffers, second_tiles, joined, active, **more)

    def hand_over(result):
        close, apart = result
        return gathered(moved(close, across(0, 0)), moved(apart, across(2, 0)), 1)

    parts_zero = first_layer(after(start, second[0]), 0, True, cost=LAG)
    parts_one = first_layer(after(later, parts_zero), 0, True)
    zero = second_layer(parts_zero, 0, parts_one, cost=LAG)
    one = second_layer(parts_one, 0, zero)
    parts_zero = first_layer(after(hand_over(zero), one), 1, False, cost=LAG)
    parts_one = first_layer(after(hand_over(one), parts_zero), 1, False)
    settled = second_layer(parts_zero, 1, parts_one, final="plain", cost=LAG)
    last = second_layer(parts_one, 1, settled, final="plain", cost=TAIL)[0]
    return jnp.where(lax.axis_index("section") == 0, moved(settled[0], across(0, 1)), last)[None]


def from_behind(value, axis, steps):
    count = lax.axis_size(axis)
    pairs = [(source, (source + steps) % count) for source in range(count)]
    return lax.ppermute(value, axis, pairs)


def swapped(block, axis, distance):
    count = lax.axis_size(axis)
    route = []
    for low in range(count):
        high = low | 1 << distance
        if high != low and high < count:
            route += [(low, high), (high, low)]
    return lax.ppermute(block, axis, route)


def passed_along(array, axis, by):
    size = lax.axis_size(axis)
    pairs = [(i, i + by) for i in range(size) if 0 <= i + by < size]
    return lax.ppermute(array, axis, pairs)


def order_tiles(tiles, link_table):
    block_count = tiles.shape[0]
    radix_len = link_table.shape[1]
    tile_size = tiles.shape[2]
    inverse = jnp.argsort(link_table, axis=1)
    shaped = tiles.reshape(block_count, radix_len, tile_size, tile_size)
    ordered = jnp.take_along_axis(shaped, inverse[:, :, None, None], axis=1)
    return ordered.reshape(block_count, radix_len * tile_size, tile_size)


def mixed_layer(group_rows, ordered, bias_row):
    block_count = ordered.shape[0]
    tile_size = ordered.shape[2]
    row_count = group_rows.shape[1]
    summed = jnp.einsum("bkc,kr->bcr", ordered, group_rows, preferred_element_type=jnp.float32)
    summed = summed.reshape(block_count * tile_size, row_count) + bias_row[:, None]
    return jnp.clip(summed, 0.0, CEILING).astype(jnp.bfloat16)


def rotate_slots(slot_store):
    return from_behind(slot_store, "section", 1)


def general_body(inputs, weight_first, weight_second, bias_first, bias_second, links_first, links_second):
    section_count = lax.axis_size("section")
    section_here = lax.axis_index("section")
    owner_parity = lax.axis_index("owners") % 2
    slot_store = inputs[0]
    row_count = slot_store.shape[1]
    owner_width = slot_store.shape[0]
    zeros_own = jnp.zeros((owner_width, row_count), jnp.bfloat16)
    full_first, full_second = (
        lax.all_gather(weight_first, "rep", axis=1, tiled=True),
        lax.all_gather(weight_second, "rep", axis=1, tiled=True),
    )
    first_tiles = order_tiles(full_first[0], links_first[0])
    second_tiles = order_tiles(full_second[0], links_second[0])
    handed = zeros_own
    tick_total = 2 * section_count - 1
    for tick_index in range(tick_total):
        if tick_index < section_count:
            incoming = jnp.where(section_here == 0, slot_store, handed)
        else:
            incoming = handed
        active = jnp.logical_and(
            section_here <= tick_index, section_here > tick_index - section_count
        )
        own_half = lax.all_to_all(incoming, "owners", split_axis=0, concat_axis=0, tiled=True)
        other_half = swapped(own_half, "owners", 0)
        lower_half = jnp.where(owner_parity == 0, own_half, other_half)
        upper_half = jnp.where(owner_parity == 0, other_half, own_half)
        apply_group_rows = jnp.concatenate([lower_half, upper_half], axis=0)
        middle = lax.cond(
            active,
            lambda: mixed_layer(apply_group_rows, first_tiles, bias_first[0]),
            lambda: zeros_own,
        )
        regrouped = lax.all_to_all(middle, "owners", split_axis=0, concat_axis=0, tiled=True)
        group_rows = regrouped
        result = lax.cond(
            active, lambda: mixed_layer(group_rows, second_tiles, bias_second[0]), lambda: zeros_own
        )
        if tick_index >= section_count - 1:
            slot_store = jnp.where(section_here == section_count - 1, result, slot_store)
        if tick_index < tick_total - 1:
            handed = passed_along(result, "section", 1)
        slot_store = rotate_slots(slot_store)
    slot_store = rotate_slots(slot_store)
    return slot_store[None]


def body(*arrays):
    inputs, weight_first = arrays[:2]
    owner_count = lax.axis_size("owners")
    size = weight_first.shape[3]
    width = inputs.shape[1]
    fits = (
        lax.axis_size("section") == 2
        and lax.axis_size("rep") == 2
        and owner_count == 4
        and width == 2 * size * owner_count
        and weight_first.shape[2] == 2 * width
        and arrays[2].shape[2] == width
    )
    return fast_body(*arrays) if fits else general_body(*arrays)


def solution(mesh):
    placed = (
        P("section", "owners", ("groups", "rep")),
        P("section", ("owners", "rep"), None, None),
        P("section", ("owners", "rep"), None, None),
        P("section", "owners"),
        P("section", "owners"),
        P("section", "owners", None),
        P("section", "owners", None),
    )
    return jax.shard_map(
        body,
        mesh=mesh,
        in_specs=placed,
        out_specs=P("section", "owners", ("groups", "rep")),
        check_vma=False,
    )
```

```python
import functools

import jax
import jax.numpy as jnp
from jax import lax
from jax.experimental import pallas as pl
from jax.experimental.pallas import tpu as pltpu
from jax.sharding import PartitionSpec as P

CEILING = 4.0
LAG = 1
TAIL = 10**10


def place_tiles(links, source, ordered, first):
    owner_count = ordered.shape[0]
    owner_bits = owner_count.bit_length() - 1
    me = lax.axis_index("owners")
    half, _, size = source.shape
    slots = links.shape[1]
    two_parts = slots > 2 * owner_count
    flip = me * 4 + (me & 1) * 2 if two_parts else me * 2
    for block in range(half):
        row = first + block
        distance = (row >> 1) ^ me
        for slot in range(slots):
            place = links[row, slot]
            if two_parts:
                key = ((place & (2 * owner_count - 2)) << 1) | ((place >> (owner_bits + 1)) << 1) | (place & 1)
            else:
                key = place
            low = pl.multiple_of((key ^ flip) * size, size)
            ordered[distance, pl.ds(low, size), pl.ds(block % 2 * size, size)] = source[
                block, pl.ds(slot * size, size), :
            ]


def order_other_kernel(links, other_tiles, ordered):
    place_tiles(links, other_tiles, ordered, (1 - lax.axis_index("rep")) * other_tiles.shape[0])


def order_own_kernel(links, own_tiles, bias, half_ordered, ordered, shifts):
    place_tiles(links, own_tiles, ordered, lax.axis_index("rep") * own_tiles.shape[0])
    size = own_tiles.shape[2]
    for distance in range(shifts.shape[0]):
        for j in range(2):
            row = 2 * (lax.axis_index("owners") ^ distance) + j
            shifts[pl.ds(distance, 1), pl.ds(j * size, size)] = bias[pl.ds(row, 1), :]


def order_weights(links, own_tiles, other_tiles, bias):
    half, depth, size = own_tiles.shape
    vmem = pl.BlockSpec(memory_space=pltpu.VMEM)
    smem = pl.BlockSpec(memory_space=pltpu.SMEM)
    ordered = jax.ShapeDtypeStruct((half, depth, 2 * size), jnp.bfloat16)
    common = dict(
        compiler_params=pltpu.CompilerParams(vmem_limit_bytes=24 * 2**20),
        cost_estimate=pl.CostEstimate(flops=1, bytes_accessed=1, transcendentals=0),
    )
    half_ordered = pl.pallas_call(
        order_other_kernel, out_shape=ordered, in_specs=[smem, vmem], out_specs=vmem, **common
    )(links, other_tiles)
    return pl.pallas_call(
        order_own_kernel,
        out_shape=[ordered, jax.ShapeDtypeStruct((half, 2 * size), jnp.float32)],
        in_specs=[smem, vmem, vmem, vmem],
        out_specs=[vmem, vmem],
        input_output_aliases={3: 0},
        **common,
    )(links, own_tiles, bias, half_ordered)


def layer_kernel(tile_list, out_groups, raw, final, active_section, stage, *refs):
    ordered, shifts = refs[:2]
    buffer_count = 1 + max(buffer for buffer, _, _ in tile_list)
    buffers = refs[2 : 2 + buffer_count]
    rest = list(refs[2 + buffer_count :])
    settled = rest.pop(0) if final == "merge" else None
    out_count = 1 if final or stage == "begin" else len(out_groups)
    outs = rest[:out_count]
    turned = rest[out_count] if raw else None
    section = lax.axis_index("section")
    me = lax.axis_index("owners")
    width = ordered.shape[2]

    def run():
        if raw:
            for place, (buffer, column, _) in enumerate(tile_list):
                turned[place] = buffers[buffer][pl.ds(column, width), :].T
        for distance in reversed(range(ordered.shape[0])):
            total = shifts[distance] if stage == "rest" else shifts[pl.ds(distance, 1), :]
            for place, (buffer, column, key) in enumerate(tile_list):
                left = turned[place] if raw else buffers[buffer][:, pl.ds(column, width)]
                if raw:
                    key = (key & ~1) + ((key & 1) ^ (me & 1))
                low = pl.multiple_of(key * width, width) if raw else key * width
                right = ordered[distance, pl.ds(low, width), :]
                total = total + jnp.dot(left, right, preferred_element_type=jnp.float32)
            if stage == "begin":
                outs[0][distance] = total
                continue
            value = jnp.clip(total, 0.0, CEILING).astype(jnp.bfloat16)
            if final:
                outs[0][pl.ds(pl.multiple_of((me ^ distance) * width, width), width), :] = value.T
            else:
                for out, group in zip(outs, out_groups, strict=True):
                    if distance in group:
                        out[:, pl.ds(group.index(distance) * width, width)] = value

    pl.when(section == active_section)(run)
    if final == "merge":

        @pl.when(section != active_section)
        def _():
            outs[0][...] = settled[...]


def layer(ordered, shifts, buffers, tile_list, out_groups, active_section, raw=False, final=None, settled=None, cost=1, stage=None):
    count, depth, width = ordered.shape
    rows = buffers[0].shape[1] if raw else buffers[0].shape[0]
    if stage == "begin":
        shapes = [jax.ShapeDtypeStruct((count, rows, width), jnp.float32)]
    elif final:
        shapes = [jax.ShapeDtypeStruct((count * width, rows), jnp.bfloat16)]
    else:
        shapes = [jax.ShapeDtypeStruct((rows, len(group) * width), jnp.bfloat16) for group in out_groups]
    vmem = pl.BlockSpec(memory_space=pltpu.VMEM)
    operands = [ordered, shifts, *buffers] + ([settled] if final == "merge" else [])
    return pl.pallas_call(
        functools.partial(layer_kernel, tile_list, out_groups, raw, final, active_section, stage),
        out_shape=shapes,
        in_specs=[vmem] * len(operands),
        out_specs=[vmem] * len(shapes),
        scratch_shapes=[pltpu.VMEM((len(tile_list), rows, width), jnp.bfloat16)] if raw else [],
        compiler_params=pltpu.CompilerParams(vmem_limit_bytes=16 * 2**20),
        cost_estimate=pl.CostEstimate(flops=cost, bytes_accessed=1, transcendentals=0),
    )(*operands)


def fast_body(inputs, weight_first, weight_second, bias_first, bias_second, links_first, links_second):
    owner_count = lax.axis_size("owners")
    me = lax.axis_index("owners")
    size = weight_first.shape[3]
    features = inputs[0]
    piece = features.shape[0] // owner_count

    def moved(value, route):
        pairs = []
        for owner in range(owner_count):
            for place in range(2):
                for core in range(2):
                    to_owner, to_place, to_core = route(owner, place, core)
                    pairs.append(((owner * 2 + place) * 2 + core, (to_owner * 2 + to_place) * 2 + to_core))
        return lax.ppermute(value, ("owners", "section", "rep"), pairs)

    def within(distance, section):
        return lambda owner, place, core: (owner ^ distance, place, core) if place == section else (owner, place, 1 - core)

    def across(distance, section):
        return lambda owner, place, core: (owner ^ distance if place == section else owner, 1 - place, 1 - core)

    def other_core(value):
        return lax.ppermute(value, "rep", [(0, 1), (1, 0)])

    halves = features.reshape(2, 2 * piece, features.shape[1])
    near = lax.dynamic_index_in_dim(halves, me // 2, 0, keepdims=False)
    far = lax.dynamic_index_in_dim(halves, 1 - me // 2, 0, keepdims=False)
    def after(value, *others):
        return lax.optimization_barrier((value, *others))[0]

    def gathered(close, apart, section):
        beside = within(1, section)
        return [close, moved(close, beside), apart, moved(apart, beside)]

    first_own, second_own = weight_first[0], weight_second[0]
    first_other = other_core(first_own)
    far_two, near_one = moved(far, within(2, 0)), moved(near, within(1, 0))
    crossed_far = moved(far, across(2, 1))
    crossed_near = [moved(near, across(distance, 1)) for distance in (0, 1)]
    first = order_weights(links_first[0], first_own, first_other, bias_first[0].reshape(-1, size))
    second_other = other_core(second_own)
    second = order_weights(links_second[0], second_own, second_other, bias_second[0].reshape(-1, size))
    start = [near, near_one, far_two, moved(after(far_two, first[0]), within(1, 0))]
    later = [*crossed_near, crossed_far, moved(after(crossed_far, second[0]), within(1, 0))]

    raw_tiles = [(buffer, column * piece, 2 * buffer + column) for buffer in range(4) for column in range(2)]
    order = [(0, 0), (0, 1), (1, 1), (1, 0), (2, 0), (2, 1), (3, 1), (3, 0)]
    later_tiles = [(place // 2, place % 2 * piece, 2 * sender + part) for place, (sender, part) in enumerate(order)]
    second_tiles = [(buffer, 0, buffer) for buffer in range(4)]

    apart = [[0], [1], [2], [3]]
    joined = [[0, 1], [2, 3]]

    def first_layer(buffers, active, raw, cost=1):
        spots = raw_tiles if raw else later_tiles
        return layer(*first, buffers, spots, apart, active, raw=raw, cost=cost)

    def second_layer(parts, active, earlier, **more):
        arrived = {distance: moved(parts[distance], within(distance, active)) for distance in (2, 1, 3)}
        buffers = after([parts[0]] + [arrived[distance] for distance in range(1, owner_count)], earlier)
        return layer(*second, buffers, second_tiles, joined, active, **more)

    def hand_over(result):
        close, apart = result
        return gathered(moved(close, across(0, 0)), moved(apart, across(2, 0)), 1)

    parts_zero = first_layer(after(start, second[0]), 0, True, cost=LAG)
    parts_one = first_layer(after(later, parts_zero), 0, True)
    def handed_layer(buffers, earlier, cost=1):
        *ready, last = buffers
        begun = layer(*first, after(ready, earlier), later_tiles[:6], apart, 1, stage="begin")[0]
        rest = [(0, column, key) for _, column, key in later_tiles[6:]]
        return layer(first[0], begun, [last], rest, apart, 1, cost=cost, stage="rest")

    zero = second_layer(parts_zero, 0, parts_one, cost=LAG)
    one = second_layer(parts_one, 0, zero)
    parts_zero = handed_layer(hand_over(zero), one, cost=LAG)
    parts_one = handed_layer(hand_over(one), parts_zero)
    settled = second_layer(parts_zero, 1, parts_one, final="plain", cost=LAG)
    last = second_layer(parts_one, 1, settled, final="plain", cost=TAIL)[0]
    return jnp.where(lax.axis_index("section") == 0, moved(settled[0], across(0, 1)), last)[None]


def from_behind(value, axis, steps):
    count = lax.axis_size(axis)
    pairs = [(source, (source + steps) % count) for source in range(count)]
    return lax.ppermute(value, axis, pairs)


def swapped(block, axis, distance):
    count = lax.axis_size(axis)
    route = []
    for low in range(count):
        high = low | 1 << distance
        if high != low and high < count:
            route += [(low, high), (high, low)]
    return lax.ppermute(block, axis, route)


def passed_along(array, axis, by):
    size = lax.axis_size(axis)
    pairs = [(i, i + by) for i in range(size) if 0 <= i + by < size]
    return lax.ppermute(array, axis, pairs)


def order_tiles(tiles, link_table):
    block_count = tiles.shape[0]
    radix_len = link_table.shape[1]
    tile_size = tiles.shape[2]
    inverse = jnp.argsort(link_table, axis=1)
    shaped = tiles.reshape(block_count, radix_len, tile_size, tile_size)
    ordered = jnp.take_along_axis(shaped, inverse[:, :, None, None], axis=1)
    return ordered.reshape(block_count, radix_len * tile_size, tile_size)


def mixed_layer(group_rows, ordered, bias_row):
    block_count = ordered.shape[0]
    tile_size = ordered.shape[2]
    row_count = group_rows.shape[1]
    summed = jnp.einsum("bkc,kr->bcr", ordered, group_rows, preferred_element_type=jnp.float32)
    summed = summed.reshape(block_count * tile_size, row_count) + bias_row[:, None]
    return jnp.clip(summed, 0.0, CEILING).astype(jnp.bfloat16)


def rotate_slots(slot_store):
    return from_behind(slot_store, "section", 1)


def general_body(inputs, weight_first, weight_second, bias_first, bias_second, links_first, links_second):
    section_count = lax.axis_size("section")
    section_here = lax.axis_index("section")
    owner_parity = lax.axis_index("owners") % 2
    slot_store = inputs[0]
    row_count = slot_store.shape[1]
    owner_width = slot_store.shape[0]
    zeros_own = jnp.zeros((owner_width, row_count), jnp.bfloat16)
    full_first, full_second = (
        lax.all_gather(weight_first, "rep", axis=1, tiled=True),
        lax.all_gather(weight_second, "rep", axis=1, tiled=True),
    )
    first_tiles = order_tiles(full_first[0], links_first[0])
    second_tiles = order_tiles(full_second[0], links_second[0])
    handed = zeros_own
    tick_total = 2 * section_count - 1
    for tick_index in range(tick_total):
        if tick_index < section_count:
            incoming = jnp.where(section_here == 0, slot_store, handed)
        else:
            incoming = handed
        active = jnp.logical_and(
            section_here <= tick_index, section_here > tick_index - section_count
        )
        own_half = lax.all_to_all(incoming, "owners", split_axis=0, concat_axis=0, tiled=True)
        other_half = swapped(own_half, "owners", 0)
        lower_half = jnp.where(owner_parity == 0, own_half, other_half)
        upper_half = jnp.where(owner_parity == 0, other_half, own_half)
        apply_group_rows = jnp.concatenate([lower_half, upper_half], axis=0)
        middle = lax.cond(
            active,
            lambda: mixed_layer(apply_group_rows, first_tiles, bias_first[0]),
            lambda: zeros_own,
        )
        regrouped = lax.all_to_all(middle, "owners", split_axis=0, concat_axis=0, tiled=True)
        group_rows = regrouped
        result = lax.cond(
            active, lambda: mixed_layer(group_rows, second_tiles, bias_second[0]), lambda: zeros_own
        )
        if tick_index >= section_count - 1:
            slot_store = jnp.where(section_here == section_count - 1, result, slot_store)
        if tick_index < tick_total - 1:
            handed = passed_along(result, "section", 1)
        slot_store = rotate_slots(slot_store)
    slot_store = rotate_slots(slot_store)
    return slot_store[None]


def body(*arrays):
    inputs, weight_first = arrays[:2]
    owner_count = lax.axis_size("owners")
    size = weight_first.shape[3]
    width = inputs.shape[1]
    fits = (
        lax.axis_size("section") == 2
        and lax.axis_size("rep") == 2
        and owner_count == 4
        and width == 2 * size * owner_count
        and weight_first.shape[2] == 2 * width
        and arrays[2].shape[2] == width
    )
    return fast_body(*arrays) if fits else general_body(*arrays)


def solution(mesh):
    placed = (
        P("section", "owners", ("groups", "rep")),
        P("section", ("owners", "rep"), None, None),
        P("section", ("owners", "rep"), None, None),
        P("section", "owners"),
        P("section", "owners"),
        P("section", "owners", None),
        P("section", "owners", None),
    )
    return jax.shard_map(
        body,
        mesh=mesh,
        in_specs=placed,
        out_specs=P("section", "owners", ("groups", "rep")),
        check_vma=False,
    )
```

```python
import functools

import jax
import jax.numpy as jnp
from jax import lax
from jax.experimental import pallas as pl
from jax.experimental.pallas import tpu as pltpu
from jax.sharding import PartitionSpec as P

CEILING = 4.0
LAG = 1
TAIL = 10**10


def place_tiles(links, source, ordered, first):
    owner_count = ordered.shape[0]
    owner_bits = owner_count.bit_length() - 1
    me = lax.axis_index("owners")
    half, _, size = source.shape
    slots = links.shape[1]
    two_parts = slots > 2 * owner_count
    flip = me * 4 + (me & 1) * 2 if two_parts else me * 2
    for block in range(half):
        row = first + block
        distance = (row >> 1) ^ me
        for slot in range(slots):
            place = links[row, slot]
            if two_parts:
                key = ((place & (2 * owner_count - 2)) << 1) | ((place >> (owner_bits + 1)) << 1) | (place & 1)
            else:
                key = place
            low = pl.multiple_of((key ^ flip) * size, size)
            ordered[distance, pl.ds(low, size), pl.ds(block % 2 * size, size)] = source[
                block, pl.ds(slot * size, size), :
            ]


def order_other_kernel(links, other_tiles, ordered):
    place_tiles(links, other_tiles, ordered, (1 - lax.axis_index("rep")) * other_tiles.shape[0])


def order_own_kernel(links, own_tiles, bias, half_ordered, ordered, shifts):
    place_tiles(links, own_tiles, ordered, lax.axis_index("rep") * own_tiles.shape[0])
    size = own_tiles.shape[2]
    for distance in range(shifts.shape[0]):
        for j in range(2):
            row = 2 * (lax.axis_index("owners") ^ distance) + j
            shifts[pl.ds(distance, 1), pl.ds(j * size, size)] = bias[pl.ds(row, 1), :]


def order_weights(links, own_tiles, other_tiles, bias):
    half, depth, size = own_tiles.shape
    vmem = pl.BlockSpec(memory_space=pltpu.VMEM)
    smem = pl.BlockSpec(memory_space=pltpu.SMEM)
    ordered = jax.ShapeDtypeStruct((half, depth, 2 * size), jnp.bfloat16)
    common = dict(
        compiler_params=pltpu.CompilerParams(vmem_limit_bytes=24 * 2**20),
        cost_estimate=pl.CostEstimate(flops=1, bytes_accessed=1, transcendentals=0),
    )
    half_ordered = pl.pallas_call(
        order_other_kernel, out_shape=ordered, in_specs=[smem, vmem], out_specs=vmem, **common
    )(links, other_tiles)
    return pl.pallas_call(
        order_own_kernel,
        out_shape=[ordered, jax.ShapeDtypeStruct((half, 2 * size), jnp.float32)],
        in_specs=[smem, vmem, vmem, vmem],
        out_specs=[vmem, vmem],
        input_output_aliases={3: 0},
        **common,
    )(links, own_tiles, bias, half_ordered)


def layer_kernel(tile_list, out_groups, raw, final, active_section, stage, *refs):
    ordered, shifts = refs[:2]
    buffer_count = 1 + max(buffer for buffer, _, _ in tile_list)
    buffers = refs[2 : 2 + buffer_count]
    rest = list(refs[2 + buffer_count :])
    settled = rest.pop(0) if final == "merge" else None
    out_count = 1 if final or stage == "begin" else len(out_groups)
    outs = rest[:out_count]
    turned = rest[out_count] if raw else None
    section = lax.axis_index("section")
    me = lax.axis_index("owners")
    width = ordered.shape[2]

    def run():
        if raw:
            for place, (buffer, column, _) in enumerate(tile_list):
                turned[place] = buffers[buffer][pl.ds(column, width), :].T
        for distance in reversed(range(ordered.shape[0])):
            total = shifts[distance] if stage == "rest" else shifts[pl.ds(distance, 1), :]
            for place, (buffer, column, key) in enumerate(tile_list):
                left = turned[place] if raw else buffers[buffer][:, pl.ds(column, width)]
                if raw:
                    key = (key & ~1) + ((key & 1) ^ (me & 1))
                low = pl.multiple_of(key * width, width) if raw else key * width
                right = ordered[distance, pl.ds(low, width), :]
                total = total + jnp.dot(left, right, preferred_element_type=jnp.float32)
            if stage == "begin":
                outs[0][distance] = total
                continue
            value = jnp.clip(total, 0.0, CEILING).astype(jnp.bfloat16)
            if final:
                outs[0][pl.ds(pl.multiple_of((me ^ distance) * width, width), width), :] = value.T
            else:
                for out, group in zip(outs, out_groups, strict=True):
                    if distance in group:
                        out[:, pl.ds(group.index(distance) * width, width)] = value

    pl.when(section == active_section)(run)
    if final == "merge":

        @pl.when(section != active_section)
        def _():
            outs[0][...] = settled[...]


def layer(ordered, shifts, buffers, tile_list, out_groups, active_section, raw=False, final=None, settled=None, cost=1, stage=None):
    count, depth, width = ordered.shape
    rows = buffers[0].shape[1] if raw else buffers[0].shape[0]
    if stage == "begin":
        shapes = [jax.ShapeDtypeStruct((count, rows, width), jnp.float32)]
    elif final:
        shapes = [jax.ShapeDtypeStruct((count * width, rows), jnp.bfloat16)]
    else:
        shapes = [jax.ShapeDtypeStruct((rows, len(group) * width), jnp.bfloat16) for group in out_groups]
    vmem = pl.BlockSpec(memory_space=pltpu.VMEM)
    operands = [ordered, shifts, *buffers] + ([settled] if final == "merge" else [])
    return pl.pallas_call(
        functools.partial(layer_kernel, tile_list, out_groups, raw, final, active_section, stage),
        out_shape=shapes,
        in_specs=[vmem] * len(operands),
        out_specs=[vmem] * len(shapes),
        scratch_shapes=[pltpu.VMEM((len(tile_list), rows, width), jnp.bfloat16)] if raw else [],
        compiler_params=pltpu.CompilerParams(vmem_limit_bytes=16 * 2**20),
        cost_estimate=pl.CostEstimate(flops=cost, bytes_accessed=1, transcendentals=0),
    )(*operands)


def fast_body(inputs, weight_first, weight_second, bias_first, bias_second, links_first, links_second):
    owner_count = lax.axis_size("owners")
    me = lax.axis_index("owners")
    size = weight_first.shape[3]
    features = inputs[0]
    piece = features.shape[0] // owner_count

    def moved(value, route):
        pairs = []
        for owner in range(owner_count):
            for place in range(2):
                for core in range(2):
                    to_owner, to_place, to_core = route(owner, place, core)
                    pairs.append(((owner * 2 + place) * 2 + core, (to_owner * 2 + to_place) * 2 + to_core))
        return lax.ppermute(value, ("owners", "section", "rep"), pairs)

    def within(distance, section):
        return lambda owner, place, core: (owner ^ distance, place, core) if place == section else (owner, place, 1 - core)

    def across(distance, section):
        return lambda owner, place, core: (owner ^ distance if place == section else owner, 1 - place, 1 - core)

    def other_core(value):
        return lax.ppermute(value, "rep", [(0, 1), (1, 0)])

    halves = features.reshape(2, 2 * piece, features.shape[1])
    near = lax.dynamic_index_in_dim(halves, me // 2, 0, keepdims=False)
    far = lax.dynamic_index_in_dim(halves, 1 - me // 2, 0, keepdims=False)
    def after(value, *others):
        return lax.optimization_barrier((value, *others))[0]

    def gathered(close, apart, section):
        beside = within(1, section)
        return [close, moved(close, beside), apart, moved(apart, beside)]

    first_own, second_own = weight_first[0], weight_second[0]
    first_other = other_core(first_own)
    far_two, near_one = moved(far, within(2, 0)), moved(near, within(1, 0))
    crossed_far = moved(far, across(2, 1))
    crossed_near = [moved(near, across(distance, 1)) for distance in (0, 1)]
    first = order_weights(links_first[0], first_own, first_other, bias_first[0].reshape(-1, size))
    second_other = other_core(second_own)
    second = order_weights(links_second[0], second_own, second_other, bias_second[0].reshape(-1, size))
    start = [near, near_one, far_two, moved(after(far_two, first[0]), within(1, 0))]
    later = [*crossed_near, crossed_far, moved(after(crossed_far, second[0]), within(1, 0))]

    raw_tiles = [(buffer, column * piece, 2 * buffer + column) for buffer in range(4) for column in range(2)]
    order = [(0, 0), (0, 1), (1, 1), (1, 0), (2, 0), (2, 1), (3, 1), (3, 0)]
    later_tiles = [(place // 2, place % 2 * piece, 2 * sender + part) for place, (sender, part) in enumerate(order)]
    second_tiles = [(buffer, 0, buffer) for buffer in range(4)]

    apart = [[0], [1], [2], [3]]
    joined = [[0, 1], [2, 3]]

    def first_layer(buffers, active, raw, cost=1):
        spots = raw_tiles if raw else later_tiles
        return layer(*first, buffers, spots, apart, active, raw=raw, cost=cost)

    def second_layer(parts, active, earlier, **more):
        arrived = {distance: moved(parts[distance], within(distance, active)) for distance in (2, 1, 3)}
        buffers = after([parts[0]] + [arrived[distance] for distance in range(1, owner_count)], earlier)
        return layer(*second, buffers, second_tiles, joined, active, **more)

    def hand_over(result):
        close, apart = result
        apart = moved(apart, across(2, 0))
        return gathered(moved(close, across(0, 0)), apart, 1)

    parts_zero = first_layer(after(start, second[0]), 0, True, cost=LAG)
    parts_one = first_layer(after(later, parts_zero), 0, True)
    def handed_layer(buffers, earlier, cost=1):
        *ready, last = buffers
        begun = layer(*first, after(ready, earlier), later_tiles[:6], apart, 1, stage="begin")[0]
        rest = [(0, column, key) for _, column, key in later_tiles[6:]]
        return layer(first[0], begun, [last], rest, apart, 1, cost=cost, stage="rest")

    zero = second_layer(parts_zero, 0, parts_one, cost=LAG)
    one = second_layer(parts_one, 0, zero)
    parts_zero = handed_layer(hand_over(zero), one, cost=LAG)
    parts_one = handed_layer(hand_over(one), parts_zero)
    settled = second_layer(parts_zero, 1, parts_one, final="plain", cost=LAG)
    last = second_layer(parts_one, 1, settled, final="plain", cost=TAIL)[0]
    return jnp.where(lax.axis_index("section") == 0, moved(settled[0], across(0, 1)), last)[None]


def from_behind(value, axis, steps):
    count = lax.axis_size(axis)
    pairs = [(source, (source + steps) % count) for source in range(count)]
    return lax.ppermute(value, axis, pairs)


def swapped(block, axis, distance):
    count = lax.axis_size(axis)
    route = []
    for low in range(count):
        high = low | 1 << distance
        if high != low and high < count:
            route += [(low, high), (high, low)]
    return lax.ppermute(block, axis, route)


def passed_along(array, axis, by):
    size = lax.axis_size(axis)
    pairs = [(i, i + by) for i in range(size) if 0 <= i + by < size]
    return lax.ppermute(array, axis, pairs)


def order_tiles(tiles, link_table):
    block_count = tiles.shape[0]
    radix_len = link_table.shape[1]
    tile_size = tiles.shape[2]
    inverse = jnp.argsort(link_table, axis=1)
    shaped = tiles.reshape(block_count, radix_len, tile_size, tile_size)
    ordered = jnp.take_along_axis(shaped, inverse[:, :, None, None], axis=1)
    return ordered.reshape(block_count, radix_len * tile_size, tile_size)


def mixed_layer(group_rows, ordered, bias_row):
    block_count = ordered.shape[0]
    tile_size = ordered.shape[2]
    row_count = group_rows.shape[1]
    summed = jnp.einsum("bkc,kr->bcr", ordered, group_rows, preferred_element_type=jnp.float32)
    summed = summed.reshape(block_count * tile_size, row_count) + bias_row[:, None]
    return jnp.clip(summed, 0.0, CEILING).astype(jnp.bfloat16)


def rotate_slots(slot_store):
    return from_behind(slot_store, "section", 1)


def general_body(inputs, weight_first, weight_second, bias_first, bias_second, links_first, links_second):
    section_count = lax.axis_size("section")
    section_here = lax.axis_index("section")
    owner_parity = lax.axis_index("owners") % 2
    slot_store = inputs[0]
    row_count = slot_store.shape[1]
    owner_width = slot_store.shape[0]
    zeros_own = jnp.zeros((owner_width, row_count), jnp.bfloat16)
    full_first, full_second = (
        lax.all_gather(weight_first, "rep", axis=1, tiled=True),
        lax.all_gather(weight_second, "rep", axis=1, tiled=True),
    )
    first_tiles = order_tiles(full_first[0], links_first[0])
    second_tiles = order_tiles(full_second[0], links_second[0])
    handed = zeros_own
    tick_total = 2 * section_count - 1
    for tick_index in range(tick_total):
        if tick_index < section_count:
            incoming = jnp.where(section_here == 0, slot_store, handed)
        else:
            incoming = handed
        active = jnp.logical_and(
            section_here <= tick_index, section_here > tick_index - section_count
        )
        own_half = lax.all_to_all(incoming, "owners", split_axis=0, concat_axis=0, tiled=True)
        other_half = swapped(own_half, "owners", 0)
        lower_half = jnp.where(owner_parity == 0, own_half, other_half)
        upper_half = jnp.where(owner_parity == 0, other_half, own_half)
        apply_group_rows = jnp.concatenate([lower_half, upper_half], axis=0)
        middle = lax.cond(
            active,
            lambda: mixed_layer(apply_group_rows, first_tiles, bias_first[0]),
            lambda: zeros_own,
        )
        regrouped = lax.all_to_all(middle, "owners", split_axis=0, concat_axis=0, tiled=True)
        group_rows = regrouped
        result = lax.cond(
            active, lambda: mixed_layer(group_rows, second_tiles, bias_second[0]), lambda: zeros_own
        )
        if tick_index >= section_count - 1:
            slot_store = jnp.where(section_here == section_count - 1, result, slot_store)
        if tick_index < tick_total - 1:
            handed = passed_along(result, "section", 1)
        slot_store = rotate_slots(slot_store)
    slot_store = rotate_slots(slot_store)
    return slot_store[None]


def body(*arrays):
    inputs, weight_first = arrays[:2]
    owner_count = lax.axis_size("owners")
    size = weight_first.shape[3]
    width = inputs.shape[1]
    fits = (
        lax.axis_size("section") == 2
        and lax.axis_size("rep") == 2
        and owner_count == 4
        and width == 2 * size * owner_count
        and weight_first.shape[2] == 2 * width
        and arrays[2].shape[2] == width
    )
    return fast_body(*arrays) if fits else general_body(*arrays)


def solution(mesh):
    placed = (
        P("section", "owners", ("groups", "rep")),
        P("section", ("owners", "rep"), None, None),
        P("section", ("owners", "rep"), None, None),
        P("section", "owners"),
        P("section", "owners"),
        P("section", "owners", None),
        P("section", "owners", None),
    )
    return jax.shard_map(
        body,
        mesh=mesh,
        in_specs=placed,
        out_specs=P("section", "owners", ("groups", "rep")),
        check_vma=False,
    )
```
